256 devices in a mesh: seq: 128 (over x, y, z), tp: 2 (over core).
Axes of the slice: x: 4, y: 4, z: 8, core: 2. Of those that a mesh axis runs over, the one named last changes fastest.
Arguments:
- hidden_acts: bfloat16 [32768, 28672], P('seq', 'tp'), may hold values from -6 to 6
- out_grads: bfloat16 [32768, 8192], P('seq', 'tp'), may hold values from -6 to 6
- proj_in: bfloat16 [28672, 64], P('tp'), may hold values from -0.03125 to 0.03125
- proj_out: bfloat16 [8192, 64], P('tp'), may hold values from -0.0625 to 0.0625
- doc_lengths: int32 [128], replicated, may hold values from 1 to 1024, 32768 in all
- owner: int32 [128], replicated, may hold values from 0 to 127, each once
- queries: float32 [4096, 4096], P(('seq', 'tp')), may hold values from -0.1 to 0.1
Outputs:
- store: float32 [128, 4096], P('seq')
- scores: float32 [4096, 128], P(('seq', 'tp'))
The draws below stay inside these ranges and needn't reach their ends.
Inputs may be any that keep to these rules, and one draw needn't show every extreme that they name: Every document has its own owner. `doc_lengths`: the lengths sum to 32768.
All inputs are finite; a program needn't handle non-finite values.
Results may differ from the reference program's by a relative error of at most 0.0003.
Values sent between devices are 32-bit elements; how exact they have to be, the bound alone decides.
A program may use at most 64 MiB of HBM per device.

```python
import math
import jax
import jax.numpy as jnp
import numpy as np
from jax import lax

D = 8192
FF = 28672
R = 64
TOK_DEV = 256
TOKENS = 32768
DOCS = 128
MOST = 1024
NQ = 4096


def levels(stream_key, shape, pieces, low, largest):
    loudness, own = 1.0, jax.random.fold_in(stream_key, 6)
    for dim, shards_of in pieces:
        draws = jnp.exp(jax.random.uniform(jax.random.fold_in(own, dim), (shards_of,), jnp.float32, low / len(pieces), largest / len(pieces)))
        loudness = loudness * jnp.repeat(draws, shape[dim] // shards_of).reshape([-1 if axis == dim else 1 for axis in range(len(shape))])
    return loudness


def split_up(count, total, most, skew):
    portions = [(1 << 20) // math.isqrt(standing ** skew) + 1 for standing in range(2, count + 1)]
    spare, holding = total - most - (count - 1), [1] * (count - 1)
    while spare > 0:
        free = [i for i in range(count - 1) if holding[i] < most]
        mass, budget = sum([portions[i] for i in free]), spare
        for i in free:
            extra = min(most - holding[i], max(1, budget * portions[i] // mass), spare)
            holding[i] = holding[i] + extra
            spare = spare - extra
    return np.array([most] + holding)


def uneven_parts(own_key, number_of, total, bound, lean):
    if number_of == 2:
        one = jax.random.randint(own_key, (), max(1, total - bound), min(bound, total - 1) + 1)
        return jnp.stack([one, total - one])
    sizes = jnp.asarray(split_up(number_of, total, bound, lean), jnp.int32)
    pairs = (number_of - 1) // 2
    donor, taker = sizes[1:1 + 2 * pairs:2], sizes[2:2 + 2 * pairs:2]
    margin = jnp.minimum(donor - 1, bound - taker)
    shifted = jax.random.randint(jax.random.fold_in(own_key, 1), (pairs,), 0, 1 << 20) % (margin + 1)
    sizes = sizes.at[1:1 + 2 * pairs:2].set(donor - shifted).at[2:2 + 2 * pairs:2].set(taker + shifted)
    return sizes[jax.random.permutation(jax.random.fold_in(own_key, 2), number_of)]


def gaussian(stream_key, shape, spread, most, cuts=(), dtype=jnp.bfloat16):
    entries = jax.random.normal(stream_key, shape, jnp.float32) * spread
    if len(cuts) > 0:
        entries = levels(stream_key, shape, cuts, -0.22, 0.18) * entries
    return jnp.clip(entries, min=-most, max=most).astype(dtype)


def setup_inputs(seed: int = 0) -> dict:
    splits = jax.random.split(jax.random.key(seed), 8)
    hidden_acts = gaussian(splits[0], (TOKENS, FF), 1.0, 6.0, ((0, 128), (1, 2)))
    out_grads = gaussian(splits[1], (TOKENS, D), 1.0, 6.0, ((0, 128), (1, 2)))
    proj_in = gaussian(splits[2], (FF, R), FF ** -0.5, 0.03125, ((0, 2),))
    proj_out = gaussian(splits[3], (D, R), D ** -0.5, 0.0625, ((0, 2),))
    doc_lengths = uneven_parts(splits[4], DOCS, TOKENS, MOST, 2).astype(jnp.int32)
    owner = jax.random.permutation(splits[5], DOCS).astype(jnp.int32)
    queries = gaussian(splits[6], (NQ, R * R), 0.015625, 0.1, ((0, 256),), jnp.float32)
    return dict(hidden_acts=hidden_acts, out_grads=out_grads, proj_in=proj_in, proj_out=proj_out, doc_lengths=doc_lengths, owner=owner, queries=queries)


def reference(hidden_acts, out_grads, proj_in, proj_out, doc_lengths, owner, queries):
    left = jnp.dot(hidden_acts, proj_in, preferred_element_type=jnp.float32)
    right = jnp.dot(out_grads, proj_out, preferred_element_type=jnp.float32)
    rank = proj_in.shape[1]
    ends = jnp.cumsum(doc_lengths).astype(jnp.int32)
    starts = (ends - doc_lengths).astype(jnp.int32)
    blocks = left.shape[0] // TOK_DEV
    left_blocks = left.reshape(blocks, TOK_DEV, rank)
    right_blocks = right.reshape(blocks, TOK_DEV, rank)

    def add_block(total, inputs):
        index, lblock, rblock = inputs
        positions = (index * TOK_DEV + jnp.arange(TOK_DEV)).astype(jnp.int32)
        member = ((starts[:, None] <= positions[None, :]) & (positions[None, :] < ends[:, None])).astype(jnp.float32)
        outer = (lblock[:, :, None] * rblock[:, None, :]).reshape(TOK_DEV, rank * rank)
        return (total + jnp.dot(member, outer, precision=lax.Precision.HIGHEST), None)
    grads, _ = lax.scan(add_block, jnp.zeros((DOCS, rank * rank), jnp.float32), (jnp.arange(blocks).astype(jnp.int32), left_blocks, right_blocks))
    normed = grads / jnp.sqrt(lax.optimization_barrier(jnp.mean(grads * grads, axis=1, keepdims=True)) + 1e-06)
    route = (owner[None, :] == jnp.arange(DOCS).astype(jnp.int32)[:, None]).astype(jnp.float32)
    store = jnp.dot(route, normed, precision=lax.Precision.HIGHEST)
    scores = jnp.dot(queries, normed.T, precision=lax.Precision.HIGHEST)
    return (store, scores)
```

```python
import jax
import jax.numpy as jnp
from jax import lax
from jax.experimental import pallas as pl
from jax.experimental.pallas import tpu as pltpu
from jax.sharding import PartitionSpec as P

X, Y, Z = 4, 4, 8
RANK = 64
TOK = 256
HALF = 128
DOCS = 128
COLS = RANK * RANK
PLANE = X * Y * 2
MESH = pl.DeviceIdType.MESH
NT = (((1,), (1,)), ((), ()))
F32, BF16 = jnp.float32, jnp.bfloat16
PARTS = ((20, 20, 16), (20, 20, 12, 4))


def ring(step, size):
    return min(step, size - step)


FAR = sorted(
    [(a, b, c) for a in range(X) for b in range(Y) for c in range(2) if (a, b, c) != (0, 0, 0)],
    key=lambda o: -(ring(o[0], X) + ring(o[1], Y)),
)
FAR_Z = sorted(range(1, Z), key=lambda d: -ring(d, Z))


def split(v):
    hi = v.astype(BF16)
    return hi, (v - hi.astype(F32)).astype(BF16)


def dot(a, b):
    return jnp.dot(a, b, preferred_element_type=F32)


def kernel(
    hid, og, pin, pout, lens, owner, queries, store, scores,
    hid_v, og_v, pin_v, pout_v, q_v, acc, sib_out, sib_in, right, left, xr, xl,
    member, outer, qs, qr, qcat, part, rs, mine, ag, fs, fr,
    load_sem, sib_send, sib_recv, x_send, x_recv, z_send, z_recv,
):
    s, c = lax.axis_index("seq"), lax.axis_index("tp")
    x, y, z = s // (Y * Z), (s // Z) % Y, s % Z
    me = (x * Y + y) * 2 + c
    live = s >= 0

    def peer(o):
        x2, y2, c2 = (x + o[0]) % X, (y + o[1]) % Y, (c + o[2]) % 2
        return x2, y2, c2, (x2 * Y + y2) * 2 + c2, ((x2 * Y + y2) * Z + z, c2)

    def along_z(d):
        z2 = (z + d) % Z
        return z2, ((x * Y + y) * Z + z2, c)

    def remote(src, dst, send, recv, device):
        return pltpu.make_async_remote_copy(
            src_ref=src, dst_ref=dst, send_sem=send, recv_sem=recv, device_id=device, device_id_type=MESH
        )

    def settle(ref, sem):
        pltpu.make_async_copy(ref, ref, sem).wait()

    started = []

    def load(src, dst):
        copy = pltpu.make_async_copy(src, dst, load_sem.at[len(started)])
        copy.start()
        started.append(copy)
        return copy

    rows = [pl.ds(pl.multiple_of((1 - c) * HALF, HALF), HALF), pl.ds(pl.multiple_of(c * HALF, HALF), HALF)]
    at = [pl.ds(0, HALF), pl.ds(HALF, HALF)]
    jobs = []
    for h in range(2):
        waits = [load(pout, pout_v)] if h == 0 else []
        waits.append(load(og.at[rows[h]], og_v.at[at[h]]))
        jobs.append((waits, "r", h, 0, og.shape[1]))
    for h in range(2):
        k0 = 0
        for width in PARTS[h]:
            ks = pl.ds(k0, width * 256)
            waits = [load(pin.at[:, ks], pin_v.at[:, ks])] if h == 0 else []
            waits.append(load(hid.at[rows[h], ks], hid_v.at[at[h], ks]))
            jobs.append((waits, "l", h, k0, width * 256))
            k0 += width * 256
    q_load = load(queries, q_v)

    barrier = pltpu.get_barrier_semaphore()
    for o in FAR:
        pl.semaphore_signal(barrier, inc=1, device_id=peer(o)[4], device_id_type=MESH)
    for d in FAR_Z:
        pl.semaphore_signal(barrier, inc=1, device_id=along_z(d)[1], device_id_type=MESH)

    def project(job):
        waits, side, h, k0, width = job
        for copy in waits:
            copy.wait()

        @pl.when(live)
        def _():
            lo = h * HALF
            if side == "r":
                acc[0, lo : lo + HALF] = lax.dot_general(
                    og_v[lo : lo + HALF], pout_v[...], NT, preferred_element_type=F32
                )
            else:
                term = lax.dot_general(
                    hid_v[lo : lo + HALF, k0 : k0 + width], pin_v[:, k0 : k0 + width], NT, preferred_element_type=F32
                )
                if k0 == 0:
                    acc[1, lo : lo + HALF] = term
                else:
                    acc[1, lo : lo + HALF] += term

    def to_sibling(side):
        sib_out[side] = acc[side, 0:HALF].T
        copy = remote(sib_out.at[side], sib_in.at[side], sib_send.at[side], sib_recv.at[side], peer((0, 0, 1))[4])
        copy.start()
        return copy

    project(jobs[0])
    pl.semaphore_wait(barrier, len(FAR) + len(FAR_Z))
    sib_r = to_sibling(0)
    project(jobs[1])
    project(jobs[2])
    sib_r.wait_recv()
    right[...] = acc[0, HALF:].T + sib_in[0]
    for o in FAR:
        x2, y2, c2, slot, device = peer(o)
        remote(right.at[pl.ds(pl.multiple_of(y2 * 16, 16), 16)], xr.at[me], x_send.at[0], x_recv.at[0], device).start()
    xr[me] = right[pl.ds(pl.multiple_of(y * 16, 16), 16), :]
    first_own = 2 + len(PARTS[0])
    for job in jobs[3:first_own]:
        project(job)
    sib_l = to_sibling(1)
    for job in jobs[first_own:]:
        project(job)
    sib_l.wait_recv()
    left[...] = acc[1, HALF:].T + sib_in[1]
    for o in FAR:
        x2, y2, c2, slot, device = peer(o)
        remote(left.at[pl.ds(pl.multiple_of((2 * x2 + c2) * 8, 8), 8)], xl.at[me], x_send.at[1], x_recv.at[1], device).start()
    xl[me] = left[pl.ds(pl.multiple_of((2 * x + c) * 8, 8), 8), :]

    lane_group = lax.broadcasted_iota(jnp.int32, (16, 128), 1) // 16
    q_load.wait()
    for bi in range(8):
        rolled = []
        for p in range(4):
            block = q_v[:, (bi * 4 + p) * 128 : (bi * 4 + p + 1) * 128]
            rolled.append(block if p == 0 else pltpu.roll(block, 16 * p, 1))
        for bj in range(4):
            pick = (lane_group + (4 - bj)) % 4
            out = rolled[3]
            for p in range(3):
                out = jnp.where(pick == p, rolled[p], out)
            qs[((bi // 2) * Y + bj) * 2 + bi % 2] = out
    for o in FAR:
        slot, device = peer(o)[3:]
        remote(qs.at[slot], qr.at[me], x_send.at[2], x_recv.at[2], device).start()
    qr[me] = qs[me]

    lane = lax.broadcasted_iota(jnp.int32, (8, DOCS), 1)
    lengths = jnp.broadcast_to(lens[...], (8, DOCS))
    ends = lengths
    for shift in (1, 2, 4, 8, 16, 32, 64):
        ends = ends + jnp.where(lane >= shift, pltpu.roll(ends, shift, 1), 0)
    starts = (ends - lengths)[0:1]
    ends = ends[0:1]
    token = lax.broadcasted_iota(jnp.int32, (HALF, DOCS), 0)
    for k in range(PLANE):
        t = token + (((k // 2) * Z + z) * TOK + (k % 2) * HALF)
        inside = (starts <= t) & (t < ends)
        member[k * HALF : (k + 1) * HALF, :] = jnp.where(inside, 1.0, 0.0).astype(BF16)

    settle(xr.at[pl.ds(0, PLANE - 1)], x_recv.at[0])
    settle(xl.at[pl.ds(0, PLANE - 1)], x_recv.at[1])
    groups = [(4 * (i % 2) + y + i // 2) % 8 for i in range(8)]
    for k in range(PLANE):
        r = xr[k]
        l = xl[k]
        for i in range(8):
            hi, lo = split(l[i : i + 1, :] * r)
            outer[0, groups[i], :, k * HALF : (k + 1) * HALF] = hi
            outer[1, groups[i], :, k * HALF : (k + 1) * HALF] = lo
    both = dot(outer[...].reshape(256, PLANE * HALF), member[...])
    part[...] = both[0:128] + both[128:256]

    for d in FAR_Z:
        z2, device = along_z(d)
        remote(part.at[pl.ds(pl.multiple_of(z2 * 16, 16), 16)], rs.at[z], z_send.at[0], z_recv.at[0], device).start()
    rs[z] = part[pl.ds(pl.multiple_of(z * 16, 16), 16), :]
    settle(qr.at[pl.ds(0, PLANE - 1)], x_recv.at[2])
    for k in range(PLANE):
        hi, lo = split(qr[k])
        qcat[16 * k : 16 * k + 16, 0:128] = hi
        qcat[16 * k : 16 * k + 16, 128:256] = lo
    settle(rs.at[pl.ds(0, Z - 1)], z_recv.at[0])
    total = rs[0]
    for k in range(1, Z):
        total = total + rs[k]
    mine[...] = total
    for d in FAR_Z:
        device = along_z(d)[1]
        remote(mine, ag.at[z], z_send.at[1], z_recv.at[1], device).start()
    ag[z] = total
    chip = lax.broadcasted_iota(jnp.int32, (16, DOCS), 0)
    chosen = jnp.where(owner[...] == chip * Z + z, 1.0, 0.0).astype(BF16)
    settle(ag.at[pl.ds(0, Z - 1)], z_recv.at[1])

    grads = ag[...].reshape(128, DOCS)
    hi, lo = split(grads)
    squares = jnp.sum(grads * grads, axis=0, keepdims=True)
    partial_scores = dot(qcat[...], jnp.concatenate([hi, hi], axis=0)) + dot(qcat[:, 0:128], lo)
    row_part = lax.dot_general(chosen, hi, NT, preferred_element_type=F32) + lax.dot_general(
        chosen, lo, NT, preferred_element_type=F32
    )
    which = lax.broadcasted_iota(jnp.int32, (8, 128), 0)
    for k in range(PLANE):
        fs[k, 0:16] = partial_scores[16 * k : 16 * k + 16]
        fs[k, 16:24] = jnp.where(which == 0, squares, jnp.where(which == 1, row_part[k // 2 : k // 2 + 1], 0.0))
    for o in FAR:
        slot, device = peer(o)[3:]
        remote(fs.at[slot], fr.at[me], x_send.at[3], x_recv.at[3], device).start()
    fr[me] = fs[me]
    settle(fr.at[pl.ds(0, PLANE - 1)], x_recv.at[3])

    summed = fr[0]
    for k in range(1, PLANE):
        summed = summed + fr[k]
    inverse = 1.0 / jnp.sqrt(summed[16:17] * (1.0 / COLS) + 1e-06)
    scores[...] = summed[0:16] * inverse
    own = jnp.sum(jnp.where(owner[...] == s, inverse, 0.0), axis=1, keepdims=True)
    lanes = lax.broadcasted_iota(jnp.int32, (8, 128), 1) // 16
    tiles = [
        jnp.concatenate([fr[((bi // 2) * Y + bj) * 2 + bi % 2, 17:18, :] for bi in range(8)], axis=0) * own
        for bj in range(4)
    ]
    for p in range(4):
        pick = (lanes + (4 - p)) % 4
        out = tiles[3]
        for bj in range(3):
            out = jnp.where(pick == bj, tiles[bj], out)
        if p:
            out = pltpu.roll(out, 128 - 16 * p, 1)
        for bi in range(8):
            store[0:1, (bi * 4 + p) * 128 : (bi * 4 + p + 1) * 128] = out[bi : bi + 1]

    sib_r.wait_send()
    sib_l.wait_send()
    settle(xr.at[pl.ds(0, PLANE - 1)], x_send.at[0])
    settle(xl.at[pl.ds(0, PLANE - 1)], x_send.at[1])
    settle(qr.at[pl.ds(0, PLANE - 1)], x_send.at[2])
    settle(fr.at[pl.ds(0, PLANE - 1)], x_send.at[3])
    settle(rs.at[pl.ds(0, Z - 1)], z_send.at[0])
    settle(ag.at[pl.ds(0, Z - 1)], z_send.at[1])


def per_device(hidden_acts, out_grads, proj_in, proj_out, doc_lengths, owner, queries):
    anywhere = pl.BlockSpec(memory_space=pl.ANY)
    vmem = pl.BlockSpec(memory_space=pltpu.VMEM)
    width, model = hidden_acts.shape[1], out_grads.shape[1]
    dma = pltpu.SemaphoreType.DMA
    return pl.pallas_call(
        kernel,
        out_shape=(jax.ShapeDtypeStruct((1, COLS), F32), jax.ShapeDtypeStruct((16, DOCS), F32)),
        in_specs=[anywhere] * 4 + [vmem] * 2 + [anywhere],
        out_specs=(vmem, vmem),
        scratch_shapes=[
            pltpu.VMEM((TOK, width), BF16),
            pltpu.VMEM((TOK, model), BF16),
            pltpu.VMEM((RANK, width), BF16),
            pltpu.VMEM((RANK, model), BF16),
            pltpu.VMEM((16, COLS), F32),
            pltpu.VMEM((2, TOK, RANK), F32),
            pltpu.VMEM((2, RANK, HALF), F32),
            pltpu.VMEM((2, RANK, HALF), F32),
            pltpu.VMEM((RANK, HALF), F32),
            pltpu.VMEM((RANK, HALF), F32),
            pltpu.VMEM((PLANE, 16, HALF), F32),
            pltpu.VMEM((PLANE, 8, HALF), F32),
            pltpu.VMEM((PLANE * HALF, DOCS), BF16),
            pltpu.VMEM((2, 8, 16, PLANE * HALF), BF16),
            pltpu.VMEM((PLANE, 16, 128), F32),
            pltpu.VMEM((PLANE, 16, 128), F32),
            pltpu.VMEM((PLANE * 16, 256), BF16),
            pltpu.VMEM((128, DOCS), F32),
            pltpu.VMEM((Z, 16, DOCS), F32),
            pltpu.VMEM((16, DOCS), F32),
            pltpu.VMEM((Z, 16, DOCS), F32),
            pltpu.VMEM((PLANE, 24, DOCS), F32),
            pltpu.VMEM((PLANE, 24, DOCS), F32),
            dma((16,)),
            dma((2,)),
            dma((2,)),
            dma((4,)),
            dma((4,)),
            dma((2,)),
            dma((2,)),
        ],
        compiler_params=pltpu.CompilerParams(
            collective_id=1, has_side_effects=True, vmem_limit_bytes=56 << 20
        ),
        name="influence",
    )(hidden_acts, out_grads, proj_in.T, proj_out.T, doc_lengths[None], owner[None], queries)


def solution(mesh):
    in_specs = (
        P("seq", "tp"),
        P("seq", "tp"),
        P("tp", None),
        P("tp", None),
        P(),
        P(),
        P(("seq", "tp"), None),
    )
    out_specs = (P("seq", None), P(("seq", "tp"), None))
    return jax.shard_map(per_device, mesh=mesh, in_specs=in_specs, out_specs=out_specs, check_vma=False)
```

```python
import jax
import jax.numpy as jnp
from jax import lax
from jax.experimental import pallas as pl
from jax.experimental.pallas import tpu as pltpu
from jax.sharding import PartitionSpec as P

X, Y, Z = 4, 4, 8
RANK = 64
TOK = 256
HALF = 128
DOCS = 128
COLS = RANK * RANK
CHIPS = X * Y
MESH = pl.DeviceIdType.MESH
NT = (((1,), (1,)), ((), ()))
F32, BF16 = jnp.float32, jnp.bfloat16
PARTS = ((20, 20, 16), (20, 20, 12, 4))
PLAN = (0, 1, 2, 3, 4, "meet", "give right", "give left", 5, "send right", 6, 7, 8)


HOPS = (0, 1, 2, 1)
FAR = sorted(range(1, CHIPS), key=lambda o: -(HOPS[o >> 2] + HOPS[o & 3]))
FAR_Z = (4, 5, 7, 6, 3, 2, 1)


def split(v):
    hi = v.astype(BF16)
    return hi, (v - hi.astype(F32)).astype(BF16)


def dot(a, b):
    return jnp.dot(a, b, preferred_element_type=F32)


def kernel(
    hid, og, pin, pout, lens_in, owner_in, queries, store, scores,
    hid_v, og_v, pin_v, pout_v, lens, owner, q_v, acc, sib_out, sib_in, right, left, xr, xl,
    member, outer, qs, qr, qcat, g_out, g_in, part, rs, mine, ag, ag_sib, fs, fr,
    load_sem, sib_send, sib_recv, x_send, x_recv, z_send, z_recv,
):
    s, c = lax.axis_index("seq"), lax.axis_index("tp")
    z = s & (Z - 1)
    me = s >> 3
    x, y = me >> 2, me & 3
    live = s >= 0
    sibling = (s, 1 - c)

    def peer(o):
        chip = me ^ o
        return chip, ((chip << 3) | z, c)

    def along_z(d):
        return z ^ d, (s ^ d, c)

    def remote(src, dst, send, recv, device):
        copy = pltpu.make_async_remote_copy(
            src_ref=src, dst_ref=dst, send_sem=send, recv_sem=recv, device_id=device, device_id_type=MESH
        )
        copy.start()
        return copy

    def to_sibling(n, src, dst):
        return remote(src, dst, sib_send.at[n], sib_recv.at[n], sibling)

    def settle(ref, sem):
        pltpu.make_async_copy(ref, ref, sem).wait()

    def rows(n, size):
        return pl.ds(pl.multiple_of(n * size, size), size)

    started = []

    def load(src, dst):
        copy = pltpu.make_async_copy(src, dst, load_sem.at[len(started)])
        copy.start()
        started.append(copy)
        return copy

    barrier = pltpu.get_barrier_semaphore()

    def announce():
        for o in FAR:
            pl.semaphore_signal(barrier, inc=1, device_id=peer(o)[1], device_id_type=MESH)
        for d in FAR_Z:
            pl.semaphore_signal(barrier, inc=1, device_id=along_z(d)[1], device_id_type=MESH)
        pl.semaphore_signal(barrier, inc=1, device_id=sibling, device_id_type=MESH)

    announce()
    tokens = [rows(1 - c, HALF), rows(c, HALF)]
    jobs = []
    for h in range(2):
        waits = [load(pout, pout_v)] if h == 0 else []
        waits.append(load(og.at[tokens[h]], og_v.at[pl.ds(h * HALF, HALF)]))
        jobs.append((waits, "r", h, 0, og.shape[1]))
    for h in range(2):
        k0 = 0
        for width in PARTS[h]:
            ks = pl.ds(k0, width * 256)
            waits = [load(pin.at[:, ks], pin_v.at[:, ks])] if h == 0 else []
            waits.append(load(hid.at[tokens[h], ks], hid_v.at[pl.ds(h * HALF, HALF), ks]))
            jobs.append((waits, "l", h, k0, width * 256))
            k0 += width * 256
    last_loads = [load(lens_in, lens), load(owner_in, owner), load(queries, q_v)]

    def project(job):
        waits, side, h, k0, width = job
        for copy in waits:
            copy.wait()

        @pl.when(live)
        def _():
            lo = h * HALF
            if side == "r":
                acc[0, lo : lo + HALF] = lax.dot_general(
                    og_v[lo : lo + HALF], pout_v[...], NT, preferred_element_type=F32
                )
            else:
                term = lax.dot_general(
                    hid_v[lo : lo + HALF, k0 : k0 + width], pin_v[:, k0 : k0 + width], NT, preferred_element_type=F32
                )
                if k0 == 0:
                    acc[1, lo : lo + HALF] = term
                else:
                    acc[1, lo : lo + HALF] += term

    sib_copies = {}

    def give(side):
        sib_out[side] = acc[side, 0:HALF].T
        sib_copies[side] = to_sibling(side, sib_out.at[side], sib_in.at[side])

    def send_right():
        sib_copies[0].wait_recv()
        right[...] = acc[0, HALF:].T + sib_in[0]
        for o in FAR:
            chip, device = peer(o)
            remote(right.at[rows(chip & 3, 16)], xr.at[me], x_send.at[0], x_recv.at[0], device)
        xr[me] = right[rows(y, 16), :]

    for step in PLAN:
        if step == "meet":
            pl.semaphore_wait(barrier, len(FAR) + len(FAR_Z) + 1)
        elif step == "give right":
            give(0)
        elif step == "give left":
            give(1)
        elif step == "send right":
            send_right()
        else:
            project(jobs[step])
    sib_copies[1].wait_recv()
    left[...] = acc[1, HALF:].T + sib_in[1]
    for o in FAR:
        chip, device = peer(o)
        remote(left.at[rows(chip >> 2, 16)], xl.at[me], x_send.at[1], x_recv.at[1], device)
    xl[me] = left[rows(x, 16), :]

    lane_group = lax.broadcasted_iota(jnp.int32, (16, 128), 1) // 16
    for copy in last_loads:
        copy.wait()
    for bi in range(8):
        rolled = []
        for p in range(4):
            block = q_v[:, (bi * 4 + p) * 128 : (bi * 4 + p + 1) * 128]
            rolled.append(block if p == 0 else pltpu.roll(block, 16 * p, 1))
        for bj in range(4):
            pick = (lane_group + (4 - bj)) % 4
            out = rolled[3]
            for p in range(3):
                out = jnp.where(pick == p, rolled[p], out)
            qs[(bi // 2) * Y + bj, bi % 2] = out
    for o in FAR:
        chip, device = peer(o)
        remote(qs.at[chip], qr.at[:, me], x_send.at[2], x_recv.at[2], device)
    for half in range(2):
        qr[half, me] = qs[me, half]

    lane = lax.broadcasted_iota(jnp.int32, (8, DOCS), 1)
    lengths = jnp.broadcast_to(lens[...], (8, DOCS))
    ends = lengths
    for shift in (1, 2, 4, 8, 16, 32, 64):
        ends = ends + jnp.where(lane >= shift, pltpu.roll(ends, shift, 1), 0)
    starts = (ends - lengths)[0:1]
    ends = ends[0:1]
    token = lax.broadcasted_iota(jnp.int32, (HALF, DOCS), 0) + (z * TOK + c * HALF)
    for k in range(CHIPS):
        t = token + k * (Z * TOK)
        inside = (starts <= t) & (t < ends)
        member[k * HALF : (k + 1) * HALF, :] = jnp.where(inside, 1.0, 0.0).astype(BF16)

    settle(xr.at[pl.ds(0, CHIPS - 1)], x_recv.at[0])
    settle(xl.at[pl.ds(0, CHIPS - 1)], x_recv.at[1])
    groups = [(4 * (i % 2) + y + i // 2) & 7 for i in range(8)]

    def sums(half, n):
        for k in range(CHIPS):
            r = xr[k]
            l = xl[k, rows(half, 8), :]
            for i in range(8):
                hi, lo = split(l[i : i + 1, :] * r)
                outer[n, 0, groups[i], :, k * HALF : (k + 1) * HALF] = hi
                outer[n, 1, groups[i], :, k * HALF : (k + 1) * HALF] = lo
        both = dot(outer[n].reshape(256, CHIPS * HALF), member[...])
        return both[0:128] + both[128:256]

    g_out[...] = sums(1 - c, 0)
    g_copy = to_sibling(2, g_out, g_in)
    own_sums = sums(c, 1)
    g_copy.wait_recv()
    part[...] = own_sums + g_in[...]

    for d in FAR_Z:
        z2, device = along_z(d)
        remote(part.at[rows(z2, 16)], rs.at[z], z_send.at[0], z_recv.at[0], device)
    rs[z] = part[rows(z, 16), :]

    settle(qr.at[:, pl.ds(0, CHIPS - 1)], x_recv.at[2])
    for n, half in enumerate((c, 1 - c)):
        for k in range(CHIPS):
            hi, lo = split(qr[half, k])
            qcat[n, 16 * k : 16 * k + 16, 0:128] = hi
            qcat[n, 16 * k : 16 * k + 16, 128:256] = lo
    settle(rs.at[pl.ds(0, Z - 1)], z_recv.at[0])
    total = rs[0]
    for k in range(1, Z):
        total = total + rs[k]
    mine[...] = total
    for d in FAR_Z:
        device = along_z(d)[1]
        remote(mine, ag.at[z], z_send.at[1], z_recv.at[1], device)
    ag[z] = total
    chip_row = lax.broadcasted_iota(jnp.int32, (CHIPS, DOCS), 0)
    chosen = jnp.where(owner[...] == chip_row * Z + z, 1.0, 0.0).astype(BF16)
    settle(ag.at[pl.ds(0, Z - 1)], z_recv.at[1])

    ag_copy = to_sibling(3, ag, ag_sib)

    def score(n, table):
        grads = table[...].reshape(128, DOCS)
        hi, lo = split(grads)
        row_part = lax.dot_general(chosen, hi, NT, preferred_element_type=F32) + lax.dot_general(
            chosen, lo, NT, preferred_element_type=F32
        )
        part_scores = dot(qcat[n], jnp.concatenate([hi, hi], axis=0)) + dot(qcat[n, :, 0:128], lo)
        return part_scores, jnp.sum(grads * grads, axis=0, keepdims=True), row_part

    own_scores, own_squares, own_row = score(0, ag)
    ag_copy.wait_recv()
    sib_scores, sib_squares, sib_row = score(1, ag_sib)
    both_scores = own_scores + sib_scores
    squares = own_squares + sib_squares
    first_core = c == 0
    row_0 = jnp.where(first_core, own_row, sib_row)
    row_1 = jnp.where(first_core, sib_row, own_row)
    for k in range(CHIPS):
        fs[k, 0:16] = both_scores[16 * k : 16 * k + 16]
        fs[k, 16:17] = squares
        fs[k, 17:18] = row_0[k : k + 1]
        fs[k, 18:19] = row_1[k : k + 1]
    for o in FAR:
        chip, device = peer(o)
        remote(fs.at[chip], fr.at[me], x_send.at[3], x_recv.at[3], device)
    fr[me] = fs[me]
    settle(fr.at[pl.ds(0, CHIPS - 1)], x_recv.at[3])

    summed = fr[0]
    for k in range(1, CHIPS):
        summed = summed + fr[k]
    inverse = 1.0 / jnp.sqrt(summed[16:17] * (1.0 / COLS) + 1e-06)
    scores[...] = summed[0:16] * inverse
    own = jnp.sum(jnp.where(owner[...] == s, inverse, 0.0), axis=1, keepdims=True)
    lanes = lax.broadcasted_iota(jnp.int32, (8, 128), 1) // 16
    tiles = [
        jnp.concatenate([fr[(bi // 2) * Y + bj, 17 + bi % 2 : 18 + bi % 2, :] for bi in range(8)], axis=0) * own
        for bj in range(4)
    ]
    for p in range(4):
        pick = (lanes + (4 - p)) % 4
        out = tiles[3]
        for bj in range(3):
            out = jnp.where(pick == bj, tiles[bj], out)
        if p:
            out = pltpu.roll(out, 128 - 16 * p, 1)
        for bi in range(8):
            store[0:1, (bi * 4 + p) * 128 : (bi * 4 + p + 1) * 128] = out[bi : bi + 1]

    for copy in (sib_copies[0], sib_copies[1], g_copy, ag_copy):
        copy.wait_send()
    settle(xr.at[pl.ds(0, CHIPS - 1)], x_send.at[0])
    settle(xl.at[pl.ds(0, CHIPS - 1)], x_send.at[1])
    settle(qr.at[:, pl.ds(0, CHIPS - 1)], x_send.at[2])
    settle(fr.at[pl.ds(0, CHIPS - 1)], x_send.at[3])
    settle(rs.at[pl.ds(0, Z - 1)], z_send.at[0])
    settle(ag.at[pl.ds(0, Z - 1)], z_send.at[1])


def finish(row, partial, store, scores):
    store[...] = row[...]
    scores[...] = partial[...]


def per_device(hidden_acts, out_grads, proj_in, proj_out, doc_lengths, owner, queries):
    anywhere = pl.BlockSpec(memory_space=pl.ANY)
    vmem = pl.BlockSpec(memory_space=pltpu.VMEM)
    width, model = hidden_acts.shape[1], out_grads.shape[1]
    dma = pltpu.SemaphoreType.DMA
    row, partial = pl.pallas_call(
        kernel,
        out_shape=(jax.ShapeDtypeStruct((1, COLS), F32), jax.ShapeDtypeStruct((16, DOCS), F32)),
        in_specs=[anywhere] * 7,
        out_specs=(vmem, vmem),
        scratch_shapes=[
            pltpu.VMEM((TOK, width), BF16),
            pltpu.VMEM((TOK, model), BF16),
            pltpu.VMEM((RANK, width), BF16),
            pltpu.VMEM((RANK, model), BF16),
            pltpu.VMEM((1, DOCS), jnp.int32),
            pltpu.VMEM((1, DOCS), jnp.int32),
            pltpu.VMEM((16, COLS), F32),
            pltpu.VMEM((2, TOK, RANK), F32),
            pltpu.VMEM((2, RANK, HALF), F32),
            pltpu.VMEM((2, RANK, HALF), F32),
            pltpu.VMEM((RANK, HALF), F32),
            pltpu.VMEM((RANK, HALF), F32),
            pltpu.VMEM((CHIPS, 16, HALF), F32),
            pltpu.VMEM((CHIPS, 16, HALF), F32),
            pltpu.VMEM((CHIPS * HALF, DOCS), BF16),
            pltpu.VMEM((2, 2, 8, 16, CHIPS * HALF), BF16),
            pltpu.VMEM((CHIPS, 2, 16, 128), F32),
            pltpu.VMEM((2, CHIPS, 16, 128), F32),
            pltpu.VMEM((2, CHIPS * 16, 256), BF16),
            pltpu.VMEM((128, DOCS), F32),
            pltpu.VMEM((128, DOCS), F32),
            pltpu.VMEM((128, DOCS), F32),
            pltpu.VMEM((Z, 16, DOCS), F32),
            pltpu.VMEM((16, DOCS), F32),
            pltpu.VMEM((Z, 16, DOCS), F32),
            pltpu.VMEM((Z, 16, DOCS), F32),
            pltpu.VMEM((CHIPS, 19, DOCS), F32),
            pltpu.VMEM((CHIPS, 19, DOCS), F32),
            dma((18,)),
            dma((4,)),
            dma((4,)),
            dma((4,)),
            dma((4,)),
            dma((2,)),
            dma((2,)),
        ],
        compiler_params=pltpu.CompilerParams(
            collective_id=1, has_side_effects=True, vmem_limit_bytes=56 << 20
        ),
        name="influence",
    )(hidden_acts, out_grads, proj_in.T, proj_out.T, doc_lengths[None], owner[None], queries)
    return pl.pallas_call(
        finish,
        out_shape=(jax.ShapeDtypeStruct(row.shape, F32), jax.ShapeDtypeStruct(partial.shape, F32)),
        in_specs=[vmem] * 2,
        out_specs=(vmem, vmem),
        name="finish",
    )(row, partial)


def solution(mesh):
    in_specs = (
        P("seq", "tp"),
        P("seq", "tp"),
        P("tp", None),
        P("tp", None),
        P(),
        P(),
        P(("seq", "tp"), None),
    )
    out_specs = (P("seq", None), P(("seq", "tp"), None))
    return jax.shard_map(per_device, mesh=mesh, in_specs=in_specs, out_specs=out_specs, check_vma=False)
```

```python
import jax
import jax.numpy as jnp
from jax import lax
from jax.experimental import pallas as pl
from jax.experimental.pallas import tpu as pltpu
from jax.sharding import PartitionSpec as P

X, Y, Z = 4, 4, 8
RANK = 64
TOK = 256
HALF = 128
DOCS = 128
COLS = RANK * RANK
CHIPS = X * Y
MESH = pl.DeviceIdType.MESH
NT = (((1,), (1,)), ((), ()))
F32, BF16 = jnp.float32, jnp.bfloat16
PARTS = ((20, 20, 16), (20, 20, 12, 4))
PLAN = (0, 1, 2, 3, 4, "meet", "give right", "give left", 5, "send right", 6, 7, 8)


HOPS = (0, 1, 2, 1)
FAR = sorted(range(1, CHIPS), key=lambda o: -(HOPS[o >> 2] + HOPS[o & 3]))
FAR_Z = (4, 5, 7, 6, 3, 2, 1)


def split(v):
    hi = v.astype(BF16)
    return hi, (v - hi.astype(F32)).astype(BF16)


def dot(a, b):
    return jnp.dot(a, b, preferred_element_type=F32)


def kernel(
    hid, og, pin, pout, lens_in, owner_in, queries, store, scores,
    hid_v, og_v, pin_v, pout_v, lens, owner, q_v, acc, sib_out, sib_in, right, left, xr, xl,
    member, outer, qs, qr, qcat, g_out, g_in, part, rs, mine, ag, ag_sib, fs, fr,
    load_sem, sib_send, sib_recv, x_send, x_recv, z_send, z_recv,
):
    s, c = lax.axis_index("seq"), lax.axis_index("tp")
    z = s & (Z - 1)
    me = s >> 3
    x, y = me >> 2, me & 3
    live = s >= 0
    sibling = (s, 1 - c)

    def peer(o):
        chip = me ^ o
        return chip, ((chip << 3) | z, c)

    def along_z(d):
        return z ^ d, (s ^ d, c)

    def remote(src, dst, send, recv, device):
        copy = pltpu.make_async_remote_copy(
            src_ref=src, dst_ref=dst, send_sem=send, recv_sem=recv, device_id=device, device_id_type=MESH
        )
        copy.start()
        return copy

    def to_sibling(n, src, dst):
        return remote(src, dst, sib_send.at[n], sib_recv.at[n], sibling)

    def settle(ref, sem):
        pltpu.make_async_copy(ref, ref, sem).wait()

    def rows(n, size):
        return pl.ds(pl.multiple_of(n * size, size), size)

    started = []

    def load(src, dst):
        copy = pltpu.make_async_copy(src, dst, load_sem.at[len(started)])
        copy.start()
        started.append(copy)
        return copy

    barrier = pltpu.get_barrier_semaphore()

    def announce():
        for o in FAR:
            pl.semaphore_signal(barrier, inc=1, device_id=peer(o)[1], device_id_type=MESH)
        for d in FAR_Z:
            pl.semaphore_signal(barrier, inc=1, device_id=along_z(d)[1], device_id_type=MESH)
        pl.semaphore_signal(barrier, inc=1, device_id=sibling, device_id_type=MESH)

    tokens = [rows(1 - c, HALF), rows(c, HALF)]
    jobs = []
    for h in range(2):
        waits = [load(pout, pout_v)] if h == 0 else []
        waits.append(load(og.at[tokens[h]], og_v.at[pl.ds(h * HALF, HALF)]))
        jobs.append((waits, "r", h, 0, og.shape[1]))
    for h in range(2):
        k0 = 0
        for width in PARTS[h]:
            ks = pl.ds(k0, width * 256)
            waits = [load(pin.at[:, ks], pin_v.at[:, ks])] if h == 0 else []
            waits.append(load(hid.at[tokens[h], ks], hid_v.at[pl.ds(h * HALF, HALF), ks]))
            jobs.append((waits, "l", h, k0, width * 256))
            k0 += width * 256
            if len(jobs) == 3:
                announce()
    last_loads = [load(lens_in, lens), load(owner_in, owner), load(queries, q_v)]

    def project(job):
        waits, side, h, k0, width = job
        for copy in waits:
            copy.wait()

        @pl.when(live)
        def _():
            lo = h * HALF
            if side == "r":
                acc[0, lo : lo + HALF] = lax.dot_general(
                    og_v[lo : lo + HALF], pout_v[...], NT, preferred_element_type=F32
                )
            else:
                term = lax.dot_general(
                    hid_v[lo : lo + HALF, k0 : k0 + width], pin_v[:, k0 : k0 + width], NT, preferred_element_type=F32
                )
                if k0 == 0:
                    acc[1, lo : lo + HALF] = term
                else:
                    acc[1, lo : lo + HALF] += term

    sib_copies = {}

    def give(side):
        sib_out[side] = acc[side, 0:HALF].T
        sib_copies[side] = to_sibling(side, sib_out.at[side], sib_in.at[side])

    def send_right():
        sib_copies[0].wait_recv()
        right[...] = acc[0, HALF:].T + sib_in[0]
        for o in FAR:
            chip, device = peer(o)
            remote(right.at[rows(chip & 3, 16)], xr.at[me], x_send.at[0], x_recv.at[0], device)
        xr[me] = right[rows(y, 16), :]

    for step in PLAN:
        if step == "meet":
            pl.semaphore_wait(barrier, len(FAR) + len(FAR_Z) + 1)
        elif step == "give right":
            give(0)
        elif step == "give left":
            give(1)
        elif step == "send right":
            send_right()
        else:
            project(jobs[step])
    sib_copies[1].wait_recv()
    left[...] = acc[1, HALF:].T + sib_in[1]
    for o in FAR:
        chip, device = peer(o)
        remote(left.at[rows(chip >> 2, 16)], xl.at[me], x_send.at[1], x_recv.at[1], device)
    xl[me] = left[rows(x, 16), :]

    lane_group = lax.broadcasted_iota(jnp.int32, (16, 128), 1) // 16
    for copy in last_loads:
        copy.wait()
    for bi in range(8):
        rolled = []
        for p in range(4):
            block = q_v[:, (bi * 4 + p) * 128 : (bi * 4 + p + 1) * 128]
            rolled.append(block if p == 0 else pltpu.roll(block, 16 * p, 1))
        for bj in range(4):
            pick = (lane_group + (4 - bj)) % 4
            out = rolled[3]
            for p in range(3):
                out = jnp.where(pick == p, rolled[p], out)
            qs[(bi // 2) * Y + bj, bi % 2] = out
    for o in FAR:
        chip, device = peer(o)
        remote(qs.at[chip], qr.at[:, me], x_send.at[2], x_recv.at[2], device)
    for half in range(2):
        qr[half, me] = qs[me, half]

    lane = lax.broadcasted_iota(jnp.int32, (8, DOCS), 1)
    lengths = jnp.broadcast_to(lens[...], (8, DOCS))
    ends = lengths
    for shift in (1, 2, 4, 8, 16, 32, 64):
        ends = ends + jnp.where(lane >= shift, pltpu.roll(ends, shift, 1), 0)
    starts = (ends - lengths)[0:1]
    ends = ends[0:1]
    token = lax.broadcasted_iota(jnp.int32, (HALF, DOCS), 0) + (z * TOK + c * HALF)
    for k in range(CHIPS):
        t = token + k * (Z * TOK)
        inside = (starts <= t) & (t < ends)
        member[k * HALF : (k + 1) * HALF, :] = jnp.where(inside, 1.0, 0.0).astype(BF16)

    settle(xr.at[pl.ds(0, CHIPS - 1)], x_recv.at[0])
    settle(xl.at[pl.ds(0, CHIPS - 1)], x_recv.at[1])
    groups = [(4 * (i % 2) + y + i // 2) & 7 for i in range(8)]

    def sums(half, n):
        for k in range(CHIPS):
            r = xr[k]
            l = xl[k, rows(half, 8), :]
            for i in range(8):
                hi, lo = split(l[i : i + 1, :] * r)
                outer[n, 0, groups[i], :, k * HALF : (k + 1) * HALF] = hi
                outer[n, 1, groups[i], :, k * HALF : (k + 1) * HALF] = lo
        both = dot(outer[n].reshape(256, CHIPS * HALF), member[...])
        return both[0:128] + both[128:256]

    g_out[...] = sums(1 - c, 0)
    g_copy = to_sibling(2, g_out, g_in)
    own_sums = sums(c, 1)
    g_copy.wait_recv()
    part[...] = own_sums + g_in[...]

    for d in FAR_Z:
        z2, device = along_z(d)
        remote(part.at[rows(z2, 16)], rs.at[z], z_send.at[0], z_recv.at[0], device)
    rs[z] = part[rows(z, 16), :]

    settle(qr.at[:, pl.ds(0, CHIPS - 1)], x_recv.at[2])
    for n, half in enumerate((c, 1 - c)):
        for k in range(CHIPS):
            hi, lo = split(qr[half, k])
            qcat[n, 16 * k : 16 * k + 16, 0:128] = hi
            qcat[n, 16 * k : 16 * k + 16, 128:256] = lo
    settle(rs.at[pl.ds(0, Z - 1)], z_recv.at[0])
    total = rs[0]
    for k in range(1, Z):
        total = total + rs[k]
    mine[...] = total
    for d in FAR_Z:
        device = along_z(d)[1]
        remote(mine, ag.at[z], z_send.at[1], z_recv.at[1], device)
    ag[z] = total
    chip_row = lax.broadcasted_iota(jnp.int32, (CHIPS, DOCS), 0)
    chosen = jnp.where(owner[...] == chip_row * Z + z, 1.0, 0.0).astype(BF16)
    settle(ag.at[pl.ds(0, Z - 1)], z_recv.at[1])

    ag_copy = to_sibling(3, ag, ag_sib)

    def score(n, table):
        grads = table[...].reshape(128, DOCS)
        hi, lo = split(grads)
        row_part = lax.dot_general(chosen, hi, NT, preferred_element_type=F32) + lax.dot_general(
            chosen, lo, NT, preferred_element_type=F32
        )
        part_scores = dot(qcat[n], jnp.concatenate([hi, hi], axis=0)) + dot(qcat[n, :, 0:128], lo)
        return part_scores, jnp.sum(grads * grads, axis=0, keepdims=True), row_part

    own_scores, own_squares, own_row = score(0, ag)
    ag_copy.wait_recv()
    sib_scores, sib_squares, sib_row = score(1, ag_sib)
    both_scores = own_scores + sib_scores
    squares = own_squares + sib_squares
    first_core = c == 0
    row_0 = jnp.where(first_core, own_row, sib_row)
    row_1 = jnp.where(first_core, sib_row, own_row)
    for k in range(CHIPS):
        fs[k, 0:16] = both_scores[16 * k : 16 * k + 16]
        fs[k, 16:17] = squares
        fs[k, 17:18] = row_0[k : k + 1]
        fs[k, 18:19] = row_1[k : k + 1]
    for o in FAR:
        chip, device = peer(o)
        remote(fs.at[chip], fr.at[me], x_send.at[3], x_recv.at[3], device)
    fr[me] = fs[me]
    settle(fr.at[pl.ds(0, CHIPS - 1)], x_recv.at[3])

    summed = fr[0]
    for k in range(1, CHIPS):
        summed = summed + fr[k]
    inverse = 1.0 / jnp.sqrt(summed[16:17] * (1.0 / COLS) + 1e-06)
    scores[...] = summed[0:16] * inverse
    own = jnp.sum(jnp.where(owner[...] == s, inverse, 0.0), axis=1, keepdims=True)
    lanes = lax.broadcasted_iota(jnp.int32, (8, 128), 1) // 16
    tiles = [
        jnp.concatenate([fr[(bi // 2) * Y + bj, 17 + bi % 2 : 18 + bi % 2, :] for bi in range(8)], axis=0) * own
        for bj in range(4)
    ]
    for p in range(4):
        pick = (lanes + (4 - p)) % 4
        out = tiles[3]
        for bj in range(3):
            out = jnp.where(pick == bj, tiles[bj], out)
        if p:
            out = pltpu.roll(out, 128 - 16 * p, 1)
        for bi in range(8):
            store[0:1, (bi * 4 + p) * 128 : (bi * 4 + p + 1) * 128] = out[bi : bi + 1]

    for copy in (sib_copies[0], sib_copies[1], g_copy, ag_copy):
        copy.wait_send()
    settle(xr.at[pl.ds(0, CHIPS - 1)], x_send.at[0])
    settle(xl.at[pl.ds(0, CHIPS - 1)], x_send.at[1])
    settle(qr.at[:, pl.ds(0, CHIPS - 1)], x_send.at[2])
    settle(fr.at[pl.ds(0, CHIPS - 1)], x_send.at[3])
    settle(rs.at[pl.ds(0, Z - 1)], z_send.at[0])
    settle(ag.at[pl.ds(0, Z - 1)], z_send.at[1])


def finish(row, partial, store, scores):
    store[...] = row[...]
    scores[...] = partial[...]


def per_device(hidden_acts, out_grads, proj_in, proj_out, doc_lengths, owner, queries):
    anywhere = pl.BlockSpec(memory_space=pl.ANY)
    vmem = pl.BlockSpec(memory_space=pltpu.VMEM)
    width, model = hidden_acts.shape[1], out_grads.shape[1]
    dma = pltpu.SemaphoreType.DMA
    row, partial = pl.pallas_call(
        kernel,
        out_shape=(jax.ShapeDtypeStruct((1, COLS), F32), jax.ShapeDtypeStruct((16, DOCS), F32)),
        in_specs=[anywhere] * 7,
        out_specs=(vmem, vmem),
        scratch_shapes=[
            pltpu.VMEM((TOK, width), BF16),
            pltpu.VMEM((TOK, model), BF16),
            pltpu.VMEM((RANK, width), BF16),
            pltpu.VMEM((RANK, model), BF16),
            pltpu.VMEM((1, DOCS), jnp.int32),
            pltpu.VMEM((1, DOCS), jnp.int32),
            pltpu.VMEM((16, COLS), F32),
            pltpu.VMEM((2, TOK, RANK), F32),
            pltpu.VMEM((2, RANK, HALF), F32),
            pltpu.VMEM((2, RANK, HALF), F32),
            pltpu.VMEM((RANK, HALF), F32),
            pltpu.VMEM((RANK, HALF), F32),
            pltpu.VMEM((CHIPS, 16, HALF), F32),
            pltpu.VMEM((CHIPS, 16, HALF), F32),
            pltpu.VMEM((CHIPS * HALF, DOCS), BF16),
            pltpu.VMEM((2, 2, 8, 16, CHIPS * HALF), BF16),
            pltpu.VMEM((CHIPS, 2, 16, 128), F32),
            pltpu.VMEM((2, CHIPS, 16, 128), F32),
            pltpu.VMEM((2, CHIPS * 16, 256), BF16),
            pltpu.VMEM((128, DOCS), F32),
            pltpu.VMEM((128, DOCS), F32),
            pltpu.VMEM((128, DOCS), F32),
            pltpu.VMEM((Z, 16, DOCS), F32),
            pltpu.VMEM((16, DOCS), F32),
            pltpu.VMEM((Z, 16, DOCS), F32),
            pltpu.VMEM((Z, 16, DOCS), F32),
            pltpu.VMEM((CHIPS, 19, DOCS), F32),
            pltpu.VMEM((CHIPS, 19, DOCS), F32),
            dma((18,)),
            dma((4,)),
            dma((4,)),
            dma((4,)),
            dma((4,)),
            dma((2,)),
            dma((2,)),
        ],
        compiler_params=pltpu.CompilerParams(
            collective_id=1, has_side_effects=True, vmem_limit_bytes=40 << 20
        ),
        name="influence",
    )(
        *[
            pltpu.with_memory_space_constraint(v, pltpu.HBM)
            for v in (hidden_acts, out_grads, proj_in.T, proj_out.T, doc_lengths[None], owner[None], queries)
        ]
    )
    return pl.pallas_call(
        finish,
        out_shape=(jax.ShapeDtypeStruct(row.shape, F32), jax.ShapeDtypeStruct(partial.shape, F32)),
        in_specs=[vmem] * 2,
        out_specs=(vmem, vmem),
        compiler_params=pltpu.CompilerParams(vmem_limit_bytes=1 << 20),
        name="finish",
    )(row, partial)


def solution(mesh):
    in_specs = (
        P("seq", "tp"),
        P("seq", "tp"),
        P("tp", None),
        P("tp", None),
        P(),
        P(),
        P(("seq", "tp"), None),
    )
    out_specs = (P("seq", None), P(("seq", "tp"), None))
    return jax.shard_map(per_device, mesh=mesh, in_specs=in_specs, out_specs=out_specs, check_vma=False)
```

```python
import jax
import jax.numpy as jnp
from jax import lax
from jax.experimental import pallas as pl
from jax.experimental.pallas import tpu as pltpu
from jax.sharding import PartitionSpec as P

X, Y, Z = 4, 4, 8
RANK = 64
TOK = 256
HALF = 128
DOCS = 128
COLS = RANK * RANK
CHIPS = X * Y
MESH = pl.DeviceIdType.MESH
NT = (((1,), (1,)), ((), ()))
F32, BF16 = jnp.float32, jnp.bfloat16
PARTS = ((20, 20, 16), (20, 20, 12, 4))
PLAN = (0, 1, 2, 3, 4, "meet", "give right", "give left", 5, "send right", 6, 7, 8)


HOPS = (0, 1, 2, 1)
FAR = sorted(range(1, CHIPS), key=lambda o: -(HOPS[o >> 2] + HOPS[o & 3]))
FAR_Z = (4, 5, 7, 6, 3, 2, 1)


def split(v):
    hi = v.astype(BF16)
    return hi, (v - hi.astype(F32)).astype(BF16)


def dot(a, b):
    return jnp.dot(a, b, preferred_element_type=F32)


def kernel(
    hid, og, pin, pout, lens_in, owner_in, queries, store, scores,
    hid_v, og_v, pin_v, pout_v, lens, owner, q_v, acc, sib_out, sib_in, right, left, xr, xl,
    member, outer, qs, qr, qcat, g_out, g_in, part, rs, mine, ag, ag_sib, fs, fr,
    q_first, qcat_first, f_first, fr_first,
    load_sem, sib_send, sib_recv, x_send, x_recv, z_send, z_recv, first_send, first_recv,
):
    s, c = lax.axis_index("seq"), lax.axis_index("tp")
    z = s & (Z - 1)
    me = s >> 3
    x, y = me >> 2, me & 3
    live = s >= 0
    sibling = (s, 1 - c)
    first = me == 0

    def peer(o):
        chip = me ^ o
        return chip, ((chip << 3) | z, c)

    def across(chip):
        return (chip << 3) | z, 1 - c

    def along_z(d):
        return z ^ d, (s ^ d, c)

    def remote(src, dst, send, recv, device):
        copy = pltpu.make_async_remote_copy(
            src_ref=src, dst_ref=dst, send_sem=send, recv_sem=recv, device_id=device, device_id_type=MESH
        )
        copy.start()
        return copy

    def to_sibling(n, src, dst):
        return remote(src, dst, sib_send.at[n], sib_recv.at[n], sibling)

    def settle(ref, sem):
        pltpu.make_async_copy(ref, ref, sem).wait()

    def rows(n, size):
        return pl.ds(pl.multiple_of(n * size, size), size)

    started = []

    def load(src, dst):
        copy = pltpu.make_async_copy(src, dst, load_sem.at[len(started)])
        copy.start()
        started.append(copy)
        return copy

    barrier = pltpu.get_barrier_semaphore()

    def announce():
        for o in FAR:
            pl.semaphore_signal(barrier, inc=1, device_id=peer(o)[1], device_id_type=MESH)
        for d in FAR_Z:
            pl.semaphore_signal(barrier, inc=1, device_id=along_z(d)[1], device_id_type=MESH)
        pl.semaphore_signal(barrier, inc=1, device_id=sibling, device_id_type=MESH)

        @pl.when(first)
        def _():
            for chip in range(1, CHIPS):
                pl.semaphore_signal(barrier, inc=1, device_id=across(chip), device_id_type=MESH)

        @pl.when(jnp.logical_not(first))
        def _():
            pl.semaphore_signal(barrier, inc=1, device_id=across(0), device_id_type=MESH)

    tokens = [rows(1 - c, HALF), rows(c, HALF)]
    jobs = []
    for h in range(2):
        waits = [load(pout, pout_v)] if h == 0 else []
        waits.append(load(og.at[tokens[h]], og_v.at[pl.ds(h * HALF, HALF)]))
        jobs.append((waits, "r", h, 0, og.shape[1]))
    for h in range(2):
        k0 = 0
        for width in PARTS[h]:
            ks = pl.ds(k0, width * 256)
            waits = [load(pin.at[:, ks], pin_v.at[:, ks])] if h == 0 else []
            waits.append(load(hid.at[tokens[h], ks], hid_v.at[pl.ds(h * HALF, HALF), ks]))
            jobs.append((waits, "l", h, k0, width * 256))
            k0 += width * 256
            if len(jobs) == 3:
                announce()
    last_loads = [load(lens_in, lens), load(owner_in, owner), load(queries, q_v)]

    def project(job):
        waits, side, h, k0, width = job
        for copy in waits:
            copy.wait()

        @pl.when(live)
        def _():
            lo = h * HALF
            if side == "r":
                acc[0, lo : lo + HALF] = lax.dot_general(
                    og_v[lo : lo + HALF], pout_v[...], NT, preferred_element_type=F32
                )
            else:
                term = lax.dot_general(
                    hid_v[lo : lo + HALF, k0 : k0 + width], pin_v[:, k0 : k0 + width], NT, preferred_element_type=F32
                )
                if k0 == 0:
                    acc[1, lo : lo + HALF] = term
                else:
                    acc[1, lo : lo + HALF] += term

    sib_copies = {}

    def give(side):
        sib_out[side] = acc[side, 0:HALF].T
        sib_copies[side] = to_sibling(side, sib_out.at[side], sib_in.at[side])

    def send_right():
        sib_copies[0].wait_recv()
        right[...] = acc[0, HALF:].T + sib_in[0]
        for o in FAR:
            chip, device = peer(o)
            remote(right.at[rows(chip & 3, 16)], xr.at[me], x_send.at[0], x_recv.at[0], device)
        xr[me] = right[rows(y, 16), :]

    for step in PLAN:
        if step == "meet":
            pl.semaphore_wait(barrier, len(FAR) + len(FAR_Z) + 1 + jnp.where(first, CHIPS - 1, 1))
        elif step == "give right":
            give(0)
        elif step == "give left":
            give(1)
        elif step == "send right":
            send_right()
        else:
            project(jobs[step])
    sib_copies[1].wait_recv()
    left[...] = acc[1, HALF:].T + sib_in[1]
    for o in FAR:
        chip, device = peer(o)
        remote(left.at[rows(chip >> 2, 16)], xl.at[me], x_send.at[1], x_recv.at[1], device)
    xl[me] = left[rows(x, 16), :]

    lane_group = lax.broadcasted_iota(jnp.int32, (16, 128), 1) // 16
    for copy in last_loads:
        copy.wait()
    for bi in range(8):
        rolled = []
        for p in range(4):
            block = q_v[:, (bi * 4 + p) * 128 : (bi * 4 + p + 1) * 128]
            rolled.append(block if p == 0 else pltpu.roll(block, 16 * p, 1))
        for bj in range(4):
            pick = (lane_group + (4 - bj)) % 4
            out = rolled[3]
            for p in range(3):
                out = jnp.where(pick == p, rolled[p], out)
            qs[(bi // 2) * Y + bj, bi % 2] = out
    for o in FAR:
        chip, device = peer(o)
        remote(qs.at[chip], qr.at[:, me], x_send.at[2], x_recv.at[2], device)
    for half in range(2):
        qr[half, me] = qs[me, half]

    @pl.when(first)
    def _():
        for chip in range(CHIPS):
            remote(qs.at[chip, 1 - c], q_first, first_send.at[0], first_recv.at[0], across(chip))

    lane = lax.broadcasted_iota(jnp.int32, (8, DOCS), 1)
    lengths = jnp.broadcast_to(lens[...], (8, DOCS))
    ends = lengths
    for shift in (1, 2, 4, 8, 16, 32, 64):
        ends = ends + jnp.where(lane >= shift, pltpu.roll(ends, shift, 1), 0)
    starts = (ends - lengths)[0:1]
    ends = ends[0:1]
    token = lax.broadcasted_iota(jnp.int32, (HALF, DOCS), 0) + (z * TOK + c * HALF)
    for k in range(CHIPS):
        t = token + k * (Z * TOK)
        inside = (starts <= t) & (t < ends)
        member[k * HALF : (k + 1) * HALF, :] = jnp.where(inside, 1.0, 0.0).astype(BF16)

    settle(xr.at[pl.ds(0, CHIPS - 1)], x_recv.at[0])
    settle(xl.at[pl.ds(0, CHIPS - 1)], x_recv.at[1])
    groups = [(4 * (i % 2) + y + i // 2) & 7 for i in range(8)]

    def sums(half, n):
        for k in range(CHIPS):
            r = xr[k]
            l = xl[k, rows(half, 8), :]
            for i in range(8):
                hi, lo = split(l[i : i + 1, :] * r)
                outer[n, 0, groups[i], :, k * HALF : (k + 1) * HALF] = hi
                outer[n, 1, groups[i], :, k * HALF : (k + 1) * HALF] = lo
        both = dot(outer[n].reshape(256, CHIPS * HALF), member[...])
        return both[0:128] + both[128:256]

    g_out[...] = sums(1 - c, 0)
    g_copy = to_sibling(2, g_out, g_in)
    own_sums = sums(c, 1)
    g_copy.wait_recv()
    part[...] = own_sums + g_in[...]

    for d in FAR_Z:
        z2, device = along_z(d)
        remote(part.at[rows(z2, 16)], rs.at[z], z_send.at[0], z_recv.at[0], device)
    rs[z] = part[rows(z, 16), :]

    settle(qr.at[:, pl.ds(0, CHIPS - 1)], x_recv.at[2])
    for n, half in enumerate((c, 1 - c)):
        for k in range(CHIPS):
            hi, lo = split(qr[half, k])
            qcat[n, 16 * k : 16 * k + 16, 0:128] = hi
            qcat[n, 16 * k : 16 * k + 16, 128:256] = lo
    settle(q_first, first_recv.at[0])
    for n, rows_in in enumerate((qr[c, 0], q_first[...])):
        hi, lo = split(rows_in)
        qcat_first[16 * n : 16 * n + 16, 0:128] = hi
        qcat_first[16 * n : 16 * n + 16, 128:256] = lo
    settle(rs.at[pl.ds(0, Z - 1)], z_recv.at[0])
    total = rs[0]
    for k in range(1, Z):
        total = total + rs[k]
    mine[...] = total
    for d in FAR_Z:
        device = along_z(d)[1]
        remote(mine, ag.at[z], z_send.at[1], z_recv.at[1], device)
    ag[z] = total
    chip_row = lax.broadcasted_iota(jnp.int32, (CHIPS, DOCS), 0)
    chosen = jnp.where(owner[...] == chip_row * Z + z, 1.0, 0.0).astype(BF16)
    settle(ag.at[pl.ds(0, Z - 1)], z_recv.at[1])

    ag_copy = to_sibling(3, ag, ag_sib)

    def score(n, table):
        grads = table[...].reshape(128, DOCS)
        hi, lo = split(grads)
        twice = jnp.concatenate([hi, hi], axis=0)
        row_part = lax.dot_general(chosen, hi, NT, preferred_element_type=F32) + lax.dot_general(
            chosen, lo, NT, preferred_element_type=F32
        )
        squares = jnp.sum(grads * grads, axis=0, keepdims=True)
        if n == 0:
            early = dot(qcat_first[...], twice) + dot(qcat_first[:, 0:128], lo)
            for k in range(2):
                f_first[k, 0:16] = early[16 * k : 16 * k + 16]
                f_first[k, 16:17] = squares
                f_first[k, 17:18] = row_part[0:1]
            slot = me * 2 + c

            @pl.when(first)
            def _():
                fr_first[slot] = f_first[0]

            @pl.when(jnp.logical_not(first))
            def _():
                remote(f_first.at[0], fr_first.at[slot], first_send.at[1], first_recv.at[1], (z, c))

            remote(f_first.at[1], fr_first.at[slot], first_send.at[2], first_recv.at[1], (z, 1 - c))
        part_scores = dot(qcat[n], twice) + dot(qcat[n, :, 0:128], lo)
        return part_scores, squares, row_part

    own_scores, own_squares, own_row = score(0, ag)
    ag_copy.wait_recv()
    sib_scores, sib_squares, sib_row = score(1, ag_sib)
    both_scores = own_scores + sib_scores
    squares = own_squares + sib_squares
    first_core = c == 0
    row_0 = jnp.where(first_core, own_row, sib_row)
    row_1 = jnp.where(first_core, sib_row, own_row)
    for k in range(CHIPS):
        fs[k, 0:16] = both_scores[16 * k : 16 * k + 16]
        fs[k, 16:17] = squares
        fs[k, 17:18] = row_0[k : k + 1]
        fs[k, 18:19] = row_1[k : k + 1]
    for o in FAR:
        chip, device = peer(o)

        @pl.when(me != o)
        def _():
            remote(fs.at[chip], fr.at[me], x_send.at[3], x_recv.at[3], device)

    def results(parts, row):
        summed = parts(0)
        for k in range(1, row[0]):
            summed = summed + parts(k)
        inverse = 1.0 / jnp.sqrt(summed[16:17] * (1.0 / COLS) + 1e-06)
        scores[...] = summed[0:16] * inverse
        own = jnp.sum(jnp.where(owner[...] == s, inverse, 0.0), axis=1, keepdims=True)
        lanes = lax.broadcasted_iota(jnp.int32, (8, 128), 1) // 16
        tiles = [
            jnp.concatenate([row[1]((bi // 2) * Y + bj, bi % 2) for bi in range(8)], axis=0) * own
            for bj in range(4)
        ]
        for p in range(4):
            pick = (lanes + (4 - p)) % 4
            out = tiles[3]
            for bj in range(3):
                out = jnp.where(pick == bj, tiles[bj], out)
            if p:
                out = pltpu.roll(out, 128 - 16 * p, 1)
            for bi in range(8):
                store[0:1, (bi * 4 + p) * 128 : (bi * 4 + p + 1) * 128] = out[bi : bi + 1]

    @pl.when(first)
    def _():
        settle(fr_first.at[pl.ds(0, 2 * CHIPS - 1)], first_recv.at[1])
        results(lambda k: fr_first[k], (2 * CHIPS, lambda chip, half: fr_first[2 * chip + half, 17:18, :]))
        settle(fr.at[pl.ds(0, CHIPS - 1)], x_send.at[3])
        settle(qs.at[:, 0], first_send.at[0])

    @pl.when(jnp.logical_not(first))
    def _():
        fr[me] = fs[me]
        settle(fr.at[pl.ds(0, CHIPS - 1)], x_recv.at[3])
        results(lambda k: fr[k], (CHIPS, lambda chip, half: fr[chip, 17 + half : 18 + half, :]))
        settle(fr.at[pl.ds(0, CHIPS - 2)], x_send.at[3])
        settle(f_first.at[0], first_send.at[1])

    settle(f_first.at[1], first_send.at[2])
    for copy in (sib_copies[0], sib_copies[1], g_copy, ag_copy):
        copy.wait_send()
    settle(xr.at[pl.ds(0, CHIPS - 1)], x_send.at[0])
    settle(xl.at[pl.ds(0, CHIPS - 1)], x_send.at[1])
    settle(qr.at[:, pl.ds(0, CHIPS - 1)], x_send.at[2])
    settle(rs.at[pl.ds(0, Z - 1)], z_send.at[0])
    settle(ag.at[pl.ds(0, Z - 1)], z_send.at[1])


def finish(row, partial, store, scores):
    store[...] = row[...]
    scores[...] = partial[...]


def per_device(hidden_acts, out_grads, proj_in, proj_out, doc_lengths, owner, queries):
    anywhere = pl.BlockSpec(memory_space=pl.ANY)
    vmem = pl.BlockSpec(memory_space=pltpu.VMEM)
    width, model = hidden_acts.shape[1], out_grads.shape[1]
    dma = pltpu.SemaphoreType.DMA
    row, partial = pl.pallas_call(
        kernel,
        out_shape=(jax.ShapeDtypeStruct((1, COLS), F32), jax.ShapeDtypeStruct((16, DOCS), F32)),
        in_specs=[anywhere] * 7,
        out_specs=(vmem, vmem),
        scratch_shapes=[
            pltpu.VMEM((TOK, width), BF16),
            pltpu.VMEM((TOK, model), BF16),
            pltpu.VMEM((RANK, width), BF16),
            pltpu.VMEM((RANK, model), BF16),
            pltpu.VMEM((1, DOCS), jnp.int32),
            pltpu.VMEM((1, DOCS), jnp.int32),
            pltpu.VMEM((16, COLS), F32),
            pltpu.VMEM((2, TOK, RANK), F32),
            pltpu.VMEM((2, RANK, HALF), F32),
            pltpu.VMEM((2, RANK, HALF), F32),
            pltpu.VMEM((RANK, HALF), F32),
            pltpu.VMEM((RANK, HALF), F32),
            pltpu.VMEM((CHIPS, 16, HALF), F32),
            pltpu.VMEM((CHIPS, 16, HALF), F32),
            pltpu.VMEM((CHIPS * HALF, DOCS), BF16),
            pltpu.VMEM((2, 2, 8, 16, CHIPS * HALF), BF16),
            pltpu.VMEM((CHIPS, 2, 16, 128), F32),
            pltpu.VMEM((2, CHIPS, 16, 128), F32),
            pltpu.VMEM((2, CHIPS * 16, 256), BF16),
            pltpu.VMEM((128, DOCS), F32),
            pltpu.VMEM((128, DOCS), F32),
            pltpu.VMEM((128, DOCS), F32),
            pltpu.VMEM((Z, 16, DOCS), F32),
            pltpu.VMEM((16, DOCS), F32),
            pltpu.VMEM((Z, 16, DOCS), F32),
            pltpu.VMEM((Z, 16, DOCS), F32),
            pltpu.VMEM((CHIPS, 19, DOCS), F32),
            pltpu.VMEM((CHIPS, 19, DOCS), F32),
            pltpu.VMEM((16, 128), F32),
            pltpu.VMEM((32, 256), BF16),
            pltpu.VMEM((2, 18, DOCS), F32),
            pltpu.VMEM((2 * CHIPS, 18, DOCS), F32),
            dma((18,)),
            dma((4,)),
            dma((4,)),
            dma((4,)),
            dma((4,)),
            dma((2,)),
            dma((2,)),
            dma((3,)),
            dma((2,)),
        ],
        compiler_params=pltpu.CompilerParams(
            collective_id=1, has_side_effects=True, vmem_limit_bytes=40 << 20
        ),
        name="influence",
    )(
        *[
            pltpu.with_memory_space_constraint(v, pltpu.HBM)
            for v in (hidden_acts, out_grads, proj_in.T, proj_out.T, doc_lengths[None], owner[None], queries)
        ]
    )
    return pl.pallas_call(
        finish,
        out_shape=(jax.ShapeDtypeStruct(row.shape, F32), jax.ShapeDtypeStruct(partial.shape, F32)),
        in_specs=[vmem] * 2,
        out_specs=(vmem, vmem),
        compiler_params=pltpu.CompilerParams(vmem_limit_bytes=1 << 20),
        name="finish",
    )(row, partial)


def solution(mesh):
    in_specs = (
        P("seq", "tp"),
        P("seq", "tp"),
        P("tp", None),
        P("tp", None),
        P(),
        P(),
        P(("seq", "tp"), None),
    )
    out_specs = (P("seq", None), P(("seq", "tp"), None))
    return jax.shard_map(per_device, mesh=mesh, in_specs=in_specs, out_specs=out_specs, check_vma=False)
```

```python
import jax
import jax.numpy as jnp
from jax import lax
from jax.experimental import pallas as pl
from jax.experimental.pallas import tpu as pltpu
from jax.sharding import PartitionSpec as P

X, Y, Z = 4, 4, 8
RANK = 64
TOK = 256
HALF = 128
DOCS = 128
COLS = RANK * RANK
CHIPS = X * Y
MESH = pl.DeviceIdType.MESH
NT = (((1,), (1,)), ((), ()))
F32, BF16 = jnp.float32, jnp.bfloat16
PARTS = ((20, 20, 16), (24, 24, 8))
PLAN = (0, 1, 2, 3, 4, "meet", "give right", "give left", 5, "send right", 6, 7)


HOPS = (0, 1, 2, 1)
FAR = sorted(range(1, CHIPS), key=lambda o: -(HOPS[o >> 2] + HOPS[o & 3]))
FAR_Z = (4, 5, 7, 6, 3, 2, 1)


def split(v):
    hi = v.astype(BF16)
    return hi, (v - hi.astype(F32)).astype(BF16)


def dot(a, b):
    return jnp.dot(a, b, preferred_element_type=F32)


def kernel(
    hid, og, pin, pout, lens_in, owner_in, queries, store, scores,
    hid_v, og_v, pin_v, pout_v, lens, owner, q_v, acc, sib_out, sib_in, right, left, xr, xl,
    member, outer, qs, qr, qcat, g_out, g_in, part, rs, mine, ag, ag_sib, fs, fr,
    q_first, qcat_first, f_first, fr_first,
    load_sem, sib_send, sib_recv, x_send, x_recv, z_send, z_recv, first_send, first_recv,
):
    s, c = lax.axis_index("seq"), lax.axis_index("tp")
    z = s & (Z - 1)
    me = s >> 3
    x, y = me >> 2, me & 3
    live = s >= 0
    sibling = (s, 1 - c)
    first = me == 0

    def peer(o):
        chip = me ^ o
        return chip, ((chip << 3) | z, c)

    def across(chip):
        return (chip << 3) | z, 1 - c

    def along_z(d):
        return z ^ d, (s ^ d, c)

    def remote(src, dst, send, recv, device):
        copy = pltpu.make_async_remote_copy(
            src_ref=src, dst_ref=dst, send_sem=send, recv_sem=recv, device_id=device, device_id_type=MESH
        )
        copy.start()
        return copy

    def to_sibling(n, src, dst):
        return remote(src, dst, sib_send.at[n], sib_recv.at[n], sibling)

    def settle(ref, sem):
        pltpu.make_async_copy(ref, ref, sem).wait()

    def rows(n, size):
        return pl.ds(pl.multiple_of(n * size, size), size)

    started = []

    def load(*pairs):
        sem = load_sem.at[len(started)]
        for src, dst in pairs:
            pltpu.make_async_copy(src, dst, sem).start()
        started.append(sem)
        return sem

    barrier = pltpu.get_barrier_semaphore()

    def announce():
        for o in FAR:
            pl.semaphore_signal(barrier, inc=1, device_id=peer(o)[1], device_id_type=MESH)
        for d in FAR_Z:
            pl.semaphore_signal(barrier, inc=1, device_id=along_z(d)[1], device_id_type=MESH)
        pl.semaphore_signal(barrier, inc=1, device_id=sibling, device_id_type=MESH)

        @pl.when(first)
        def _():
            for chip in range(1, CHIPS):
                pl.semaphore_signal(barrier, inc=1, device_id=across(chip), device_id_type=MESH)

        @pl.when(jnp.logical_not(first))
        def _():
            pl.semaphore_signal(barrier, inc=1, device_id=across(0), device_id_type=MESH)

    tokens = [rows(1 - c, HALF), rows(c, HALF)]
    jobs = []
    for h in range(2):
        tail = ((og.at[tokens[h]], og_v.at[pl.ds(h * HALF, HALF)]),)
        head = ((pout, pout_v),) if h == 0 else ()
        arrived = og_v.at[pl.ds(0, HALF + RANK * len(head))]
        jobs.append((load(*head, *tail), arrived, "r", h, 0, og.shape[1]))
    for h in range(2):
        k0 = 0
        for width in PARTS[h]:
            ks = pl.ds(k0, width * 256)
            tail = ((hid.at[tokens[h], ks], hid_v.at[pl.ds(h * HALF, HALF), ks]),)
            head = ((pin.at[:, ks], pin_v.at[:, ks]),) if h == 0 else ()
            arrived = hid_v.at[pl.ds(0, HALF + RANK * len(head)), ks]
            jobs.append((load(*head, *tail), arrived, "l", h, k0, width * 256))
            k0 += width * 256
            if len(jobs) == 3:
                announce()
    last_loads = [(load((a, b)), b) for a, b in ((lens_in, lens), (owner_in, owner), (queries, q_v))]

    def project(job):
        sem, arrived, side, h, k0, width = job
        settle(arrived, sem)

        @pl.when(live)
        def _():
            lo = h * HALF
            if side == "r":
                acc[0, lo : lo + HALF] = lax.dot_general(
                    og_v[lo : lo + HALF], pout_v[...], NT, preferred_element_type=F32
                )
            else:
                term = lax.dot_general(
                    hid_v[lo : lo + HALF, k0 : k0 + width], pin_v[:, k0 : k0 + width], NT, preferred_element_type=F32
                )
                if k0 == 0:
                    acc[1, lo : lo + HALF] = term
                else:
                    acc[1, lo : lo + HALF] += term

    sib_copies = {}

    def give(side):
        sib_out[side] = acc[side, 0:HALF].T
        sib_copies[side] = to_sibling(side, sib_out.at[side], sib_in.at[side])

    def send_right():
        sib_copies[0].wait_recv()
        right[...] = acc[0, HALF:].T + sib_in[0]
        for o in FAR:
            chip, device = peer(o)
            remote(right.at[rows(chip & 3, 16)], xr.at[me], x_send.at[0], x_recv.at[0], device)
        xr[me] = right[rows(y, 16), :]

    for step in PLAN:
        if step == "meet":
            pl.semaphore_wait(barrier, len(FAR) + len(FAR_Z) + 1 + jnp.where(first, CHIPS - 1, 1))
        elif step == "give right":
            give(0)
        elif step == "give left":
            give(1)
        elif step == "send right":
            send_right()
        else:
            project(jobs[step])
    sib_copies[1].wait_recv()
    left[...] = acc[1, HALF:].T + sib_in[1]
    for o in FAR:
        chip, device = peer(o)
        remote(left.at[rows(chip >> 2, 16)], xl.at[me], x_send.at[1], x_recv.at[1], device)
    xl[me] = left[rows(x, 16), :]

    lane_group = lax.broadcasted_iota(jnp.int32, (16, 128), 1) // 16
    for sem, ref in last_loads:
        settle(ref, sem)
    for bi in range(8):
        rolled = []
        for p in range(4):
            block = q_v[:, (bi * 4 + p) * 128 : (bi * 4 + p + 1) * 128]
            rolled.append(block if p == 0 else pltpu.roll(block, 16 * p, 1))
        for bj in range(4):
            pick = (lane_group + (4 - bj)) % 4
            out = rolled[3]
            for p in range(3):
                out = jnp.where(pick == p, rolled[p], out)
            qs[(bi // 2) * Y + bj, bi % 2] = out
    for o in FAR:
        chip, device = peer(o)
        remote(qs.at[chip], qr.at[:, me], x_send.at[2], x_recv.at[2], device)
    for half in range(2):
        qr[half, me] = qs[me, half]

    @pl.when(first)
    def _():
        for chip in range(CHIPS):
            remote(qs.at[chip, 1 - c], q_first, first_send.at[0], first_recv.at[0], across(chip))

    lane = lax.broadcasted_iota(jnp.int32, (8, DOCS), 1)
    lengths = jnp.broadcast_to(lens[...], (8, DOCS))
    ends = lengths
    for shift in (1, 2, 4, 8, 16, 32, 64):
        ends = ends + jnp.where(lane >= shift, pltpu.roll(ends, shift, 1), 0)
    starts = (ends - lengths)[0:1]
    ends = ends[0:1]
    token = lax.broadcasted_iota(jnp.int32, (HALF, DOCS), 0) + (z * TOK + c * HALF)
    for k in range(CHIPS):
        t = token + k * (Z * TOK)
        inside = (starts <= t) & (t < ends)
        member[k * HALF : (k + 1) * HALF, :] = jnp.where(inside, 1.0, 0.0).astype(BF16)

    settle(xr.at[pl.ds(0, CHIPS - 1)], x_recv.at[0])
    settle(xl.at[pl.ds(0, CHIPS - 1)], x_recv.at[1])
    groups = [(4 * (i % 2) + y + i // 2) & 7 for i in range(8)]

    def sums(half, n):
        for k in range(CHIPS):
            r = xr[k]
            l = xl[k, rows(half, 8), :]
            for i in range(8):
                hi, lo = split(l[i : i + 1, :] * r)
                outer[n, 0, groups[i], :, k * HALF : (k + 1) * HALF] = hi
                outer[n, 1, groups[i], :, k * HALF : (k + 1) * HALF] = lo
        both = dot(outer[n].reshape(256, CHIPS * HALF), member[...])
        return both[0:128] + both[128:256]

    g_out[...] = sums(1 - c, 0)
    g_copy = to_sibling(2, g_out, g_in)
    own_sums = sums(c, 1)
    g_copy.wait_recv()
    part[...] = own_sums + g_in[...]

    for d in FAR_Z:
        z2, device = along_z(d)
        remote(part.at[rows(z2, 16)], rs.at[z], z_send.at[0], z_recv.at[0], device)
    rs[z] = part[rows(z, 16), :]

    settle(qr.at[:, pl.ds(0, CHIPS - 1)], x_recv.at[2])
    for n, half in enumerate((c, 1 - c)):
        for k in range(CHIPS):
            hi, lo = split(qr[half, k])
            qcat[n, 16 * k : 16 * k + 16, 0:128] = hi
            qcat[n, 16 * k : 16 * k + 16, 128:256] = lo
    settle(q_first, first_recv.at[0])
    for n, rows_in in enumerate((qr[c, 0], q_first[...])):
        hi, lo = split(rows_in)
        qcat_first[16 * n : 16 * n + 16, 0:128] = hi
        qcat_first[16 * n : 16 * n + 16, 128:256] = lo
    settle(rs.at[pl.ds(0, Z - 1)], z_recv.at[0])
    total = rs[0]
    for k in range(1, Z):
        total = total + rs[k]
    mine[...] = total
    for d in FAR_Z:
        device = along_z(d)[1]
        remote(mine, ag.at[z], z_send.at[1], z_recv.at[1], device)
    ag[z] = total
    chip_row = lax.broadcasted_iota(jnp.int32, (CHIPS, DOCS), 0)
    chosen = jnp.where(owner[...] == chip_row * Z + z, 1.0, 0.0).astype(BF16)
    settle(ag.at[pl.ds(0, Z - 1)], z_recv.at[1])

    ag_copy = to_sibling(3, ag, ag_sib)

    def score(n, table):
        grads = table[...].reshape(128, DOCS)
        hi, lo = split(grads)
        twice = jnp.concatenate([hi, hi], axis=0)
        row_part = lax.dot_general(chosen, hi, NT, preferred_element_type=F32) + lax.dot_general(
            chosen, lo, NT, preferred_element_type=F32
        )
        squares = jnp.sum(grads * grads, axis=0, keepdims=True)
        if n == 0:
            early = dot(qcat_first[...], twice) + dot(qcat_first[:, 0:128], lo)
            for k in range(2):
                f_first[k, 0:16] = early[16 * k : 16 * k + 16]
                f_first[k, 16:17] = squares
                f_first[k, 17:18] = row_part[0:1]
            slot = me * 2 + c

            @pl.when(first)
            def _():
                fr_first[slot] = f_first[0]

            @pl.when(jnp.logical_not(first))
            def _():
                remote(f_first.at[0], fr_first.at[slot], first_send.at[1], first_recv.at[1], (z, c))

            remote(f_first.at[1], fr_first.at[slot], first_send.at[2], first_recv.at[1], (z, 1 - c))
        part_scores = dot(qcat[n], twice) + dot(qcat[n, :, 0:128], lo)
        return part_scores, squares, row_part

    own_scores, own_squares, own_row = score(0, ag)
    ag_copy.wait_recv()
    sib_scores, sib_squares, sib_row = score(1, ag_sib)
    both_scores = own_scores + sib_scores
    squares = own_squares + sib_squares
    first_core = c == 0
    row_0 = jnp.where(first_core, own_row, sib_row)
    row_1 = jnp.where(first_core, sib_row, own_row)
    for k in range(CHIPS):
        fs[k, 0:16] = both_scores[16 * k : 16 * k + 16]
        fs[k, 16:17] = squares
        fs[k, 17:18] = row_0[k : k + 1]
        fs[k, 18:19] = row_1[k : k + 1]
    for o in FAR:
        chip, device = peer(o)

        @pl.when(me != o)
        def _():
            remote(fs.at[chip], fr.at[me], x_send.at[3], x_recv.at[3], device)

    def results(parts, row):
        summed = parts(0)
        for k in range(1, row[0]):
            summed = summed + parts(k)
        inverse = 1.0 / jnp.sqrt(summed[16:17] * (1.0 / COLS) + 1e-06)
        scores[...] = summed[0:16] * inverse
        own = jnp.sum(jnp.where(owner[...] == s, inverse, 0.0), axis=1, keepdims=True)
        lanes = lax.broadcasted_iota(jnp.int32, (8, 128), 1) // 16
        tiles = [
            jnp.concatenate([row[1]((bi // 2) * Y + bj, bi % 2) for bi in range(8)], axis=0) * own
            for bj in range(4)
        ]
        for p in range(4):
            pick = (lanes + (4 - p)) % 4
            out = tiles[3]
            for bj in range(3):
                out = jnp.where(pick == bj, tiles[bj], out)
            if p:
                out = pltpu.roll(out, 128 - 16 * p, 1)
            for bi in range(8):
                store[0:1, (bi * 4 + p) * 128 : (bi * 4 + p + 1) * 128] = out[bi : bi + 1]

    for copy in (sib_copies[0], sib_copies[1], g_copy, ag_copy):
        copy.wait_send()
    settle(xr.at[pl.ds(0, CHIPS - 1)], x_send.at[0])
    settle(xl.at[pl.ds(0, CHIPS - 1)], x_send.at[1])
    settle(qr.at[:, pl.ds(0, CHIPS - 1)], x_send.at[2])
    settle(rs.at[pl.ds(0, Z - 1)], z_send.at[0])
    settle(ag.at[pl.ds(0, Z - 1)], z_send.at[1])
    settle(f_first.at[1], first_send.at[2])

    @pl.when(first)
    def _():
        settle(qs.at[:, 0], first_send.at[0])
        settle(fr.at[pl.ds(0, CHIPS - 1)], x_send.at[3])
        settle(fr_first.at[pl.ds(0, 2 * CHIPS - 1)], first_recv.at[1])
        results(lambda k: fr_first[k], (2 * CHIPS, lambda chip, half: fr_first[2 * chip + half, 17:18, :]))

    @pl.when(jnp.logical_not(first))
    def _():
        fr[me] = fs[me]
        settle(f_first.at[0], first_send.at[1])
        settle(fr.at[pl.ds(0, CHIPS - 2)], x_send.at[3])
        settle(fr.at[pl.ds(0, CHIPS - 1)], x_recv.at[3])
        results(lambda k: fr[k], (CHIPS, lambda chip, half: fr[chip, 17 + half : 18 + half, :]))


def finish(row, partial, store, scores):
    store[...] = row[...]
    scores[...] = partial[...]


def per_device(hidden_acts, out_grads, proj_in, proj_out, doc_lengths, owner, queries):
    anywhere = pl.BlockSpec(memory_space=pl.ANY)
    vmem = pl.BlockSpec(memory_space=pltpu.VMEM)
    width, model = hidden_acts.shape[1], out_grads.shape[1]
    dma = pltpu.SemaphoreType.DMA
    row, partial = pl.pallas_call(
        kernel,
        out_shape=(jax.ShapeDtypeStruct((1, COLS), F32), jax.ShapeDtypeStruct((16, DOCS), F32)),
        in_specs=[anywhere] * 7,
        out_specs=(vmem, vmem),
        scratch_shapes=[
            pltpu.VMEM((TOK, width), BF16),
            pltpu.VMEM((TOK, model), BF16),
            pltpu.VMEM((RANK, width), BF16),
            pltpu.VMEM((RANK, model), BF16),
            pltpu.VMEM((1, DOCS), jnp.int32),
            pltpu.VMEM((1, DOCS), jnp.int32),
            pltpu.VMEM((16, COLS), F32),
            pltpu.VMEM((2, TOK, RANK), F32),
            pltpu.VMEM((2, RANK, HALF), F32),
            pltpu.VMEM((2, RANK, HALF), F32),
            pltpu.VMEM((RANK, HALF), F32),
            pltpu.VMEM((RANK, HALF), F32),
            pltpu.VMEM((CHIPS, 16, HALF), F32),
            pltpu.VMEM((CHIPS, 16, HALF), F32),
            pltpu.VMEM((CHIPS * HALF, DOCS), BF16),
            pltpu.VMEM((2, 2, 8, 16, CHIPS * HALF), BF16),
            pltpu.VMEM((CHIPS, 2, 16, 128), F32),
            pltpu.VMEM((2, CHIPS, 16, 128), F32),
            pltpu.VMEM((2, CHIPS * 16, 256), BF16),
            pltpu.VMEM((128, DOCS), F32),
            pltpu.VMEM((128, DOCS), F32),
            pltpu.VMEM((128, DOCS), F32),
            pltpu.VMEM((Z, 16, DOCS), F32),
            pltpu.VMEM((16, DOCS), F32),
            pltpu.VMEM((Z, 16, DOCS), F32),
            pltpu.VMEM((Z, 16, DOCS), F32),
            pltpu.VMEM((CHIPS, 19, DOCS), F32),
            pltpu.VMEM((CHIPS, 19, DOCS), F32),
            pltpu.VMEM((16, 128), F32),
            pltpu.VMEM((32, 256), BF16),
            pltpu.VMEM((2, 18, DOCS), F32),
            pltpu.VMEM((2 * CHIPS, 18, DOCS), F32),
            dma((18,)),
            dma((4,)),
            dma((4,)),
            dma((4,)),
            dma((4,)),
            dma((2,)),
            dma((2,)),
            dma((3,)),
            dma((2,)),
        ],
        compiler_params=pltpu.CompilerParams(
            collective_id=1, has_side_effects=True, vmem_limit_bytes=40 << 20
        ),
        name="influence",
    )(
        *[
            pltpu.with_memory_space_constraint(v, pltpu.HBM)
            for v in (hidden_acts, out_grads, proj_in.T, proj_out.T, doc_lengths[None], owner[None], queries)
        ]
    )
    return pl.pallas_call(
        finish,
        out_shape=(jax.ShapeDtypeStruct(row.shape, F32), jax.ShapeDtypeStruct(partial.shape, F32)),
        in_specs=[vmem] * 2,
        out_specs=(vmem, vmem),
        compiler_params=pltpu.CompilerParams(vmem_limit_bytes=1 << 20),
        name="finish",
    )(row, partial)


def solution(mesh):
    in_specs = (
        P("seq", "tp"),
        P("seq", "tp"),
        P("tp", None),
        P("tp", None),
        P(),
        P(),
        P(("seq", "tp"), None),
    )
    out_specs = (P("seq", None), P(("seq", "tp"), None))
    return jax.shard_map(per_device, mesh=mesh, in_specs=in_specs, out_specs=out_specs, check_vma=False)
```

```python
import jax
import jax.numpy as jnp
from jax import lax
from jax.experimental import pallas as pl
from jax.experimental.pallas import tpu as pltpu
from jax.sharding import PartitionSpec as P

X, Y, Z = 4, 4, 8
RANK = 64
TOK = 256
HALF = 128
DOCS = 128
COLS = RANK * RANK
CHIPS = X * Y
MESH = pl.DeviceIdType.MESH
NT = (((1,), (1,)), ((), ()))
F32, BF16 = jnp.float32, jnp.bfloat16
PARTS = ((20, 20, 16), (24, 24, 8))
PLAN = (0, 1, 2, 3, 4, "meet", "give right", "give left", 5, "send right", 6, 7)


HOPS = (0, 1, 2, 1)
FAR = sorted(range(1, CHIPS), key=lambda o: -(HOPS[o >> 2] + HOPS[o & 3]))
FAR_Z = (4, 3, 5, 2, 6, 7, 1)


def split(v):
    hi = v.astype(BF16)
    return hi, (v - hi.astype(F32)).astype(BF16)


def dot(a, b):
    return jnp.dot(a, b, preferred_element_type=F32)


def kernel(
    hid, og, pin, pout, lens_in, owner_in, queries, store, scores,
    hid_v, og_v, pin_v, pout_v, lens, owner, q_v, acc, sib_out, sib_in, right, left, xr, xl,
    member, outer, qs, qr, qcat, g_out, g_in, part, rs, mine, ag, ag_sib, fs, fr,
    q_first, qcat_first, f_first, fr_first,
    load_sem, sib_send, sib_recv, x_send, x_recv, z_send, z_recv, first_send, first_recv,
):
    s, c = lax.axis_index("seq"), lax.axis_index("tp")
    z = s & (Z - 1)
    me = s >> 3
    x, y = me >> 2, me & 3
    live = s >= 0
    sibling = (s, 1 - c)
    first = (me == 0) & (c == 1)
    to_first = (z, 1)

    def peer(o):
        chip = me ^ o
        return chip, ((chip << 3) | z, c)

    def along_z(d):
        return z ^ d, (s ^ d, c)

    def remote(src, dst, send, recv, device):
        copy = pltpu.make_async_remote_copy(
            src_ref=src, dst_ref=dst, send_sem=send, recv_sem=recv, device_id=device, device_id_type=MESH
        )
        copy.start()
        return copy

    def to_sibling(n, src, dst):
        return remote(src, dst, sib_send.at[n], sib_recv.at[n], sibling)

    def settle(ref, sem):
        pltpu.make_async_copy(ref, ref, sem).wait()

    def rows(n, size):
        return pl.ds(pl.multiple_of(n * size, size), size)

    started = []

    def load(*pairs):
        sem = load_sem.at[len(started)]
        for src, dst in pairs:
            pltpu.make_async_copy(src, dst, sem).start()
        started.append(sem)
        return sem

    barrier = pltpu.get_barrier_semaphore()

    def announce():
        for o in FAR:
            pl.semaphore_signal(barrier, inc=1, device_id=peer(o)[1], device_id_type=MESH)
        for d in FAR_Z:
            pl.semaphore_signal(barrier, inc=1, device_id=along_z(d)[1], device_id_type=MESH)
        pl.semaphore_signal(barrier, inc=1, device_id=sibling, device_id_type=MESH)

        @pl.when(first)
        def _():
            for chip in range(1, CHIPS):
                pl.semaphore_signal(barrier, inc=1, device_id=((chip << 3) | z, 0), device_id_type=MESH)

        @pl.when((c == 0) & (me != 0))
        def _():
            pl.semaphore_signal(barrier, inc=1, device_id=to_first, device_id_type=MESH)

    tokens = [rows(1 - c, HALF), rows(c, HALF)]
    jobs = []
    for h in range(2):
        tail = ((og.at[tokens[h]], og_v.at[pl.ds(h * HALF, HALF)]),)
        head = ((pout, pout_v),) if h == 0 else ()
        arrived = og_v.at[pl.ds(0, HALF + RANK * len(head))]
        jobs.append((load(*head, *tail), arrived, "r", h, 0, og.shape[1]))
    for h in range(2):
        k0 = 0
        for width in PARTS[h]:
            ks = pl.ds(k0, width * 256)
            tail = ((hid.at[tokens[h], ks], hid_v.at[pl.ds(h * HALF, HALF), ks]),)
            head = ((pin.at[:, ks], pin_v.at[:, ks]),) if h == 0 else ()
            arrived = hid_v.at[pl.ds(0, HALF + RANK * len(head)), ks]
            jobs.append((load(*head, *tail), arrived, "l", h, k0, width * 256))
            k0 += width * 256
            if len(jobs) == 3:
                announce()
    last_loads = [(load((a, b)), b) for a, b in ((lens_in, lens), (owner_in, owner), (queries, q_v))]

    def project(job):
        sem, arrived, side, h, k0, width = job
        settle(arrived, sem)

        @pl.when(live)
        def _():
            lo = h * HALF
            if side == "r":
                acc[0, lo : lo + HALF] = lax.dot_general(
                    og_v[lo : lo + HALF], pout_v[...], NT, preferred_element_type=F32
                )
            else:
                term = lax.dot_general(
                    hid_v[lo : lo + HALF, k0 : k0 + width], pin_v[:, k0 : k0 + width], NT, preferred_element_type=F32
                )
                if k0 == 0:
                    acc[1, lo : lo + HALF] = term
                else:
                    acc[1, lo : lo + HALF] += term

    sib_copies = {}

    def give(side):
        sib_out[side] = acc[side, 0:HALF].T
        sib_copies[side] = to_sibling(side, sib_out.at[side], sib_in.at[side])

    def send_right():
        sib_copies[0].wait_recv()
        right[...] = acc[0, HALF:].T + sib_in[0]
        for o in FAR:
            chip, device = peer(o)
            remote(right.at[rows(chip & 3, 16)], xr.at[me], x_send.at[0], x_recv.at[0], device)
        xr[me] = right[rows(y, 16), :]

    for step in PLAN:
        if step == "meet":
            pl.semaphore_wait(barrier, len(FAR) + len(FAR_Z) + 1 + jnp.where(first, CHIPS - 1, jnp.where((c == 0) & (me != 0), 1, 0)))
        elif step == "give right":
            give(0)
        elif step == "give left":
            give(1)
        elif step == "send right":
            send_right()
        else:
            project(jobs[step])
    sib_copies[1].wait_recv()
    left[...] = acc[1, HALF:].T + sib_in[1]
    for o in FAR:
        chip, device = peer(o)
        remote(left.at[rows(chip >> 2, 16)], xl.at[me], x_send.at[1], x_recv.at[1], device)
    xl[me] = left[rows(x, 16), :]

    lane_group = lax.broadcasted_iota(jnp.int32, (16, 128), 1) // 16
    for sem, ref in last_loads:
        settle(ref, sem)
    for bi in range(8):
        rolled = []
        for p in range(4):
            block = q_v[:, (bi * 4 + p) * 128 : (bi * 4 + p + 1) * 128]
            rolled.append(block if p == 0 else pltpu.roll(block, 16 * p, 1))
        for bj in range(4):
            pick = (lane_group + (4 - bj)) % 4
            out = rolled[3]
            for p in range(3):
                out = jnp.where(pick == p, rolled[p], out)
            qs[(bi // 2) * Y + bj, bi % 2] = out
    for o in FAR:
        chip, device = peer(o)
        remote(qs.at[chip], qr.at[:, me], x_send.at[2], x_recv.at[2], device)
    for half in range(2):
        qr[half, me] = qs[me, half]

    @pl.when(first)
    def _():
        for chip in range(CHIPS):
            remote(qs.at[chip, 0], q_first, first_send.at[0], first_recv.at[0], ((chip << 3) | z, 0))

    lane = lax.broadcasted_iota(jnp.int32, (8, DOCS), 1)
    lengths = jnp.broadcast_to(lens[...], (8, DOCS))
    ends = lengths
    for shift in (1, 2, 4, 8, 16, 32, 64):
        ends = ends + jnp.where(lane >= shift, pltpu.roll(ends, shift, 1), 0)
    starts = (ends - lengths)[0:1]
    ends = ends[0:1]
    token = lax.broadcasted_iota(jnp.int32, (HALF, DOCS), 0) + (z * TOK + c * HALF)
    for k in range(CHIPS):
        t = token + k * (Z * TOK)
        inside = (starts <= t) & (t < ends)
        member[k * HALF : (k + 1) * HALF, :] = jnp.where(inside, 1.0, 0.0).astype(BF16)

    settle(xr.at[pl.ds(0, CHIPS - 1)], x_recv.at[0])
    settle(xl.at[pl.ds(0, CHIPS - 1)], x_recv.at[1])
    groups = [(4 * (i % 2) + y + i // 2) & 7 for i in range(8)]

    def sums(half, n):
        for k in range(CHIPS):
            r = xr[k]
            l = xl[k, rows(half, 8), :]
            for i in range(8):
                hi, lo = split(l[i : i + 1, :] * r)
                outer[n, 0, groups[i], :, k * HALF : (k + 1) * HALF] = hi
                outer[n, 1, groups[i], :, k * HALF : (k + 1) * HALF] = lo
        both = dot(outer[n].reshape(256, CHIPS * HALF), member[...])
        return both[0:128] + both[128:256]

    g_out[...] = sums(1 - c, 0)
    g_copy = to_sibling(2, g_out, g_in)
    own_sums = sums(c, 1)
    g_copy.wait_recv()
    part[...] = own_sums + g_in[...]

    for d in FAR_Z:
        z2, device = along_z(d)
        remote(part.at[rows(z2, 16)], rs.at[z], z_send.at[0], z_recv.at[0], device)
    rs[z] = part[rows(z, 16), :]

    settle(qr.at[:, pl.ds(0, CHIPS - 1)], x_recv.at[2])
    for n, half in enumerate((c, 1 - c)):
        for k in range(CHIPS):
            hi, lo = split(qr[half, k])
            qcat[n, 16 * k : 16 * k + 16, 0:128] = hi
            qcat[n, 16 * k : 16 * k + 16, 128:256] = lo

    @pl.when(c == 0)
    def _():
        settle(q_first, first_recv.at[0])

    @pl.when(c == 1)
    def _():
        q_first[...] = qr[1, 0]

    hi, lo = split(q_first[...])
    qcat_first[:, 0:128] = hi
    qcat_first[:, 128:256] = lo
    settle(rs.at[pl.ds(0, Z - 1)], z_recv.at[0])
    total = rs[0]
    for k in range(1, Z):
        total = total + rs[k]
    mine[...] = total
    for d in FAR_Z:
        device = along_z(d)[1]
        remote(mine, ag.at[z], z_send.at[1], z_recv.at[1], device)
    ag[z] = total
    chip_row = lax.broadcasted_iota(jnp.int32, (CHIPS, DOCS), 0)
    chosen = jnp.where(owner[...] == chip_row * Z + z, 1.0, 0.0).astype(BF16)
    settle(ag.at[pl.ds(0, Z - 1)], z_recv.at[1])

    ag_copy = to_sibling(3, ag, ag_sib)

    def score(n, table):
        grads = table[...].reshape(128, DOCS)
        hi, lo = split(grads)
        twice = jnp.concatenate([hi, hi], axis=0)
        row_part = lax.dot_general(chosen, hi, NT, preferred_element_type=F32) + lax.dot_general(
            chosen, lo, NT, preferred_element_type=F32
        )
        squares = jnp.sum(grads * grads, axis=0, keepdims=True)
        if n == 0:
            early = dot(qcat_first[...], twice) + dot(qcat_first[:, 0:128], lo)
            f_first[0:16] = early
            f_first[16:17] = squares
            f_first[17:18] = row_part[0:1]
            slot = me * 2 + c

            @pl.when(first)
            def _():
                fr_first[slot] = f_first[...]

            @pl.when(jnp.logical_not(first))
            def _():
                remote(f_first, fr_first.at[slot], first_send.at[1], first_recv.at[1], to_first)

        part_scores = dot(qcat[n], twice) + dot(qcat[n, :, 0:128], lo)
        return part_scores, squares, row_part

    own_scores, own_squares, own_row = score(0, ag)
    ag_copy.wait_recv()
    sib_scores, sib_squares, sib_row = score(1, ag_sib)
    both_scores = own_scores + sib_scores
    squares = own_squares + sib_squares
    first_core = c == 0
    row_0 = jnp.where(first_core, own_row, sib_row)
    row_1 = jnp.where(first_core, sib_row, own_row)
    for k in range(CHIPS):
        fs[k, 0:16] = both_scores[16 * k : 16 * k + 16]
        fs[k, 16:17] = squares
        fs[k, 17:18] = row_0[k : k + 1]
        fs[k, 18:19] = row_1[k : k + 1]
    for o in FAR:
        chip, device = peer(o)

        @pl.when((c == 0) | (me != o))
        def _():
            remote(fs.at[chip], fr.at[me], x_send.at[3], x_recv.at[3], device)

    def results(parts, row):
        summed = parts(0)
        for k in range(1, row[0]):
            summed = summed + parts(k)
        inverse = 1.0 / jnp.sqrt(summed[16:17] * (1.0 / COLS) + 1e-06)
        scores[...] = summed[0:16] * inverse
        own = jnp.sum(jnp.where(owner[...] == s, inverse, 0.0), axis=1, keepdims=True)
        lanes = lax.broadcasted_iota(jnp.int32, (8, 128), 1) // 16
        tiles = [
            jnp.concatenate([row[1]((bi // 2) * Y + bj, bi % 2) for bi in range(8)], axis=0) * own
            for bj in range(4)
        ]
        for p in range(4):
            pick = (lanes + (4 - p)) % 4
            out = tiles[3]
            for bj in range(3):
                out = jnp.where(pick == bj, tiles[bj], out)
            if p:
                out = pltpu.roll(out, 128 - 16 * p, 1)
            for bi in range(8):
                store[0:1, (bi * 4 + p) * 128 : (bi * 4 + p + 1) * 128] = out[bi : bi + 1]

    for copy in (sib_copies[0], sib_copies[1], g_copy, ag_copy):
        copy.wait_send()
    settle(xr.at[pl.ds(0, CHIPS - 1)], x_send.at[0])
    settle(xl.at[pl.ds(0, CHIPS - 1)], x_send.at[1])
    settle(qr.at[:, pl.ds(0, CHIPS - 1)], x_send.at[2])
    settle(rs.at[pl.ds(0, Z - 1)], z_send.at[0])
    settle(ag.at[pl.ds(0, Z - 1)], z_send.at[1])

    @pl.when(first)
    def _():
        settle(qs.at[:, 0], first_send.at[0])
        settle(fr.at[pl.ds(0, CHIPS - 1)], x_send.at[3])
        settle(fr_first.at[pl.ds(0, 2 * CHIPS - 1)], first_recv.at[1])
        results(lambda k: fr_first[k], (2 * CHIPS, lambda chip, half: fr_first[2 * chip + half, 17:18, :]))

    @pl.when(jnp.logical_not(first))
    def _():
        fr[me] = fs[me]
        settle(f_first, first_send.at[1])

        @pl.when(c == 0)
        def _():
            settle(fr.at[pl.ds(0, CHIPS - 1)], x_send.at[3])

        @pl.when(c == 1)
        def _():
            settle(fr.at[pl.ds(0, CHIPS - 2)], x_send.at[3])

        settle(fr.at[pl.ds(0, CHIPS - 1)], x_recv.at[3])
        results(lambda k: fr[k], (CHIPS, lambda chip, half: fr[chip, 17 + half : 18 + half, :]))


def finish(row, partial, store, scores):
    store[...] = row[...]
    scores[...] = partial[...]


def per_device(hidden_acts, out_grads, proj_in, proj_out, doc_lengths, owner, queries):
    anywhere = pl.BlockSpec(memory_space=pl.ANY)
    vmem = pl.BlockSpec(memory_space=pltpu.VMEM)
    width, model = hidden_acts.shape[1], out_grads.shape[1]
    dma = pltpu.SemaphoreType.DMA
    row, partial = pl.pallas_call(
        kernel,
        out_shape=(jax.ShapeDtypeStruct((1, COLS), F32), jax.ShapeDtypeStruct((16, DOCS), F32)),
        in_specs=[anywhere] * 7,
        out_specs=(vmem, vmem),
        scratch_shapes=[
            pltpu.VMEM((TOK, width), BF16),
            pltpu.VMEM((TOK, model), BF16),
            pltpu.VMEM((RANK, width), BF16),
            pltpu.VMEM((RANK, model), BF16),
            pltpu.VMEM((1, DOCS), jnp.int32),
            pltpu.VMEM((1, DOCS), jnp.int32),
            pltpu.VMEM((16, COLS), F32),
            pltpu.VMEM((2, TOK, RANK), F32),
            pltpu.VMEM((2, RANK, HALF), F32),
            pltpu.VMEM((2, RANK, HALF), F32),
            pltpu.VMEM((RANK, HALF), F32),
            pltpu.VMEM((RANK, HALF), F32),
            pltpu.VMEM((CHIPS, 16, HALF), F32),
            pltpu.VMEM((CHIPS, 16, HALF), F32),
            pltpu.VMEM((CHIPS * HALF, DOCS), BF16),
            pltpu.VMEM((2, 2, 8, 16, CHIPS * HALF), BF16),
            pltpu.VMEM((CHIPS, 2, 16, 128), F32),
            pltpu.VMEM((2, CHIPS, 16, 128), F32),
            pltpu.VMEM((2, CHIPS * 16, 256), BF16),
            pltpu.VMEM((128, DOCS), F32),
            pltpu.VMEM((128, DOCS), F32),
            pltpu.VMEM((128, DOCS), F32),
            pltpu.VMEM((Z, 16, DOCS), F32),
            pltpu.VMEM((16, DOCS), F32),
            pltpu.VMEM((Z, 16, DOCS), F32),
            pltpu.VMEM((Z, 16, DOCS), F32),
            pltpu.VMEM((CHIPS, 19, DOCS), F32),
            pltpu.VMEM((CHIPS, 19, DOCS), F32),
            pltpu.VMEM((16, 128), F32),
            pltpu.VMEM((16, 256), BF16),
            pltpu.VMEM((18, DOCS), F32),
            pltpu.VMEM((2 * CHIPS, 18, DOCS), F32),
            dma((18,)),
            dma((4,)),
            dma((4,)),
            dma((4,)),
            dma((4,)),
            dma((2,)),
            dma((2,)),
            dma((2,)),
            dma((2,)),
        ],
        compiler_params=pltpu.CompilerParams(
            collective_id=1, has_side_effects=True, vmem_limit_bytes=40 << 20
        ),
        name="influence",
    )(
        *[
            pltpu.with_memory_space_constraint(v, pltpu.HBM)
            for v in (hidden_acts, out_grads, proj_in.T, proj_out.T, doc_lengths[None], owner[None], queries)
        ]
    )
    return pl.pallas_call(
        finish,
        out_shape=(jax.ShapeDtypeStruct(row.shape, F32), jax.ShapeDtypeStruct(partial.shape, F32)),
        in_specs=[vmem] * 2,
        out_specs=(vmem, vmem),
        compiler_params=pltpu.CompilerParams(vmem_limit_bytes=1 << 20),
        name="finish",
    )(row, partial)


def solution(mesh):
    in_specs = (
        P("seq", "tp"),
        P("seq", "tp"),
        P("tp", None),
        P("tp", None),
        P(),
        P(),
        P(("seq", "tp"), None),
    )
    out_specs = (P("seq", None), P(("seq", "tp"), None))
    return jax.shard_map(per_device, mesh=mesh, in_specs=in_specs, out_specs=out_specs, check_vma=False)
```

```python
import jax
import jax.numpy as jnp
from jax import lax
from jax.experimental import pallas as pl
from jax.experimental.pallas import tpu as pltpu
from jax.sharding import PartitionSpec as P

X, Y, Z = 4, 4, 8
RANK = 64
TOK = 256
HALF = 128
DOCS = 128
COLS = RANK * RANK
CHIPS = X * Y
MESH = pl.DeviceIdType.MESH
NT = (((1,), (1,)), ((), ()))
F32, BF16 = jnp.float32, jnp.bfloat16
PARTS = ((20, 20, 16), (24, 24, 8))
PLAN = (0, 1, 2, 3, 4, "meet", "give right", "give left", 5, "send right", 6, 7)


HOPS = (0, 1, 2, 1)
FAR = sorted(range(1, CHIPS), key=lambda o: -(HOPS[o >> 2] + HOPS[o & 3]))
FAR_Z = (4, 5, 7, 6, 3, 2, 1)


def split(v):
    hi = v.astype(BF16)
    return hi, (v - hi.astype(F32)).astype(BF16)


def dot(a, b):
    return jnp.dot(a, b, preferred_element_type=F32)


def kernel(
    hid, og, pin, pout, lens_in, owner_in, queries, store, scores,
    hid_v, og_v, pin_v, pout_v, lens, owner, q_v, acc, sib_out, sib_in, right, left, xr, xl,
    member, outer, qs, qr, qcat, g_out, g_in, part, rs, mine, ag, ag_sib, fs, fr,
    q_first, qcat_first, f_first, fr_first,
    load_sem, sib_send, sib_recv, x_send, x_recv, z_send, z_recv, first_send, first_recv,
):
    s, c = lax.axis_index("seq"), lax.axis_index("tp")
    z = s & (Z - 1)
    me = s >> 3
    x, y = me >> 2, me & 3
    live = s >= 0
    sibling = (s, 1 - c)
    first = me == 0

    def peer(o):
        chip = me ^ o
        return chip, ((chip << 3) | z, c)

    def across(chip):
        return (chip << 3) | z, 1 - c

    def along_z(d):
        return z ^ d, (s ^ d, c)

    def remote(src, dst, send, recv, device):
        copy = pltpu.make_async_remote_copy(
            src_ref=src, dst_ref=dst, send_sem=send, recv_sem=recv, device_id=device, device_id_type=MESH
        )
        copy.start()
        return copy

    def to_sibling(n, src, dst):
        return remote(src, dst, sib_send.at[n], sib_recv.at[n], sibling)

    def settle(ref, sem):
        pltpu.make_async_copy(ref, ref, sem).wait()

    def rows(n, size):
        return pl.ds(pl.multiple_of(n * size, size), size)

    started = []

    def load(*pairs):
        sem = load_sem.at[len(started)]
        for src, dst in pairs:
            pltpu.make_async_copy(src, dst, sem).start()
        started.append(sem)
        return sem

    barrier = pltpu.get_barrier_semaphore()

    def announce():
        for o in FAR:
            pl.semaphore_signal(barrier, inc=1, device_id=peer(o)[1], device_id_type=MESH)
        for d in FAR_Z:
            pl.semaphore_signal(barrier, inc=1, device_id=along_z(d)[1], device_id_type=MESH)
        pl.semaphore_signal(barrier, inc=1, device_id=sibling, device_id_type=MESH)

        @pl.when(first)
        def _():
            for chip in range(1, CHIPS):
                pl.semaphore_signal(barrier, inc=1, device_id=across(chip), device_id_type=MESH)

        @pl.when(jnp.logical_not(first))
        def _():
            pl.semaphore_signal(barrier, inc=1, device_id=across(0), device_id_type=MESH)

    tokens = [rows(1 - c, HALF), rows(c, HALF)]
    jobs = []
    for h in range(2):
        tail = ((og.at[tokens[h]], og_v.at[pl.ds(h * HALF, HALF)]),)
        head = ((pout, pout_v),) if h == 0 else ()
        arrived = og_v.at[pl.ds(0, HALF + RANK * len(head))]
        jobs.append((load(*head, *tail), arrived, "r", h, 0, og.shape[1]))
    for h in range(2):
        k0 = 0
        for width in PARTS[h]:
            ks = pl.ds(k0, width * 256)
            tail = ((hid.at[tokens[h], ks], hid_v.at[pl.ds(h * HALF, HALF), ks]),)
            head = ((pin.at[:, ks], pin_v.at[:, ks]),) if h == 0 else ()
            arrived = hid_v.at[pl.ds(0, HALF + RANK * len(head)), ks]
            jobs.append((load(*head, *tail), arrived, "l", h, k0, width * 256))
            k0 += width * 256
            if len(jobs) == 3:
                announce()
    last_loads = [(load((a, b)), b) for a, b in ((lens_in, lens), (owner_in, owner), (queries, q_v))]

    def project(job):
        sem, arrived, side, h, k0, width = job
        settle(arrived, sem)

        @pl.when(live)
        def _():
            lo = h * HALF
            if side == "r":
                acc[0, lo : lo + HALF] = lax.dot_general(
                    og_v[lo : lo + HALF], pout_v[...], NT, preferred_element_type=F32
                )
            else:
                term = lax.dot_general(
                    hid_v[lo : lo + HALF, k0 : k0 + width], pin_v[:, k0 : k0 + width], NT, preferred_element_type=F32
                )
                if k0 == 0:
                    acc[1, lo : lo + HALF] = term
                else:
                    acc[1, lo : lo + HALF] += term

    sib_copies = {}

    def give(side):
        sib_out[side] = acc[side, 0:HALF].T
        sib_copies[side] = to_sibling(side, sib_out.at[side], sib_in.at[side])

    def send_right():
        sib_copies[0].wait_recv()
        right[...] = acc[0, HALF:].T + sib_in[0]
        for o in FAR:
            chip, device = peer(o)
            remote(right.at[rows(chip & 3, 16)], xr.at[me], x_send.at[0], x_recv.at[0], device)
        xr[me] = right[rows(y, 16), :]

    for step in PLAN:
        if step == "meet":
            pl.semaphore_wait(barrier, len(FAR) + len(FAR_Z) + 1 + jnp.where(first, CHIPS - 1, 1))
        elif step == "give right":
            give(0)
        elif step == "give left":
            give(1)
        elif step == "send right":
            send_right()
        else:
            project(jobs[step])
    sib_copies[1].wait_recv()
    left[...] = acc[1, HALF:].T + sib_in[1]
    for o in FAR:
        chip, device = peer(o)
        remote(left.at[rows(chip >> 2, 16)], xl.at[me], x_send.at[1], x_recv.at[1], device)
    xl[me] = left[rows(x, 16), :]

    lane_group = lax.broadcasted_iota(jnp.int32, (16, 128), 1) // 16
    for sem, ref in last_loads:
        settle(ref, sem)
    for bi in range(8):
        rolled = []
        for p in range(4):
            block = q_v[:, (bi * 4 + p) * 128 : (bi * 4 + p + 1) * 128]
            rolled.append(block if p == 0 else pltpu.roll(block, 16 * p, 1))
        for bj in range(4):
            pick = (lane_group + (4 - bj)) % 4
            out = rolled[3]
            for p in range(3):
                out = jnp.where(pick == p, rolled[p], out)
            qs[(bi // 2) * Y + bj, bi % 2] = out
    lane = lax.broadcasted_iota(jnp.int32, (8, DOCS), 1)
    lengths = jnp.broadcast_to(lens[...], (8, DOCS))
    ends = lengths
    for shift in (1, 2, 4, 8, 16, 32, 64):
        ends = ends + jnp.where(lane >= shift, pltpu.roll(ends, shift, 1), 0)
    starts = (ends - lengths)[0:1]
    ends = ends[0:1]
    token = lax.broadcasted_iota(jnp.int32, (HALF, DOCS), 0) + (z * TOK + c * HALF)
    for k in range(CHIPS):
        t = token + k * (Z * TOK)
        inside = (starts <= t) & (t < ends)
        member[k * HALF : (k + 1) * HALF, :] = jnp.where(inside, 1.0, 0.0).astype(BF16)

    settle(xr.at[pl.ds(0, CHIPS - 1)], x_recv.at[0])
    settle(xl.at[pl.ds(0, CHIPS - 1)], x_recv.at[1])
    groups = [(4 * (i % 2) + y + i // 2) & 7 for i in range(8)]

    def sums(half, n):
        for k in range(CHIPS):
            r = xr[k]
            l = xl[k, rows(half, 8), :]
            for i in range(8):
                hi, lo = split(l[i : i + 1, :] * r)
                outer[n, 0, groups[i], :, k * HALF : (k + 1) * HALF] = hi
                outer[n, 1, groups[i], :, k * HALF : (k + 1) * HALF] = lo
        both = dot(outer[n].reshape(256, CHIPS * HALF), member[...])
        return both[0:128] + both[128:256]

    g_out[...] = sums(1 - c, 0)
    g_copy = to_sibling(2, g_out, g_in)
    own_sums = sums(c, 1)
    g_copy.wait_recv()
    part[...] = own_sums + g_in[...]

    for d in FAR_Z:
        z2, device = along_z(d)
        remote(part.at[rows(z2, 16)], rs.at[z], z_send.at[0], z_recv.at[0], device)
    rs[z] = part[rows(z, 16), :]

    for o in FAR:
        chip, device = peer(o)
        remote(qs.at[chip], qr.at[:, me], x_send.at[2], x_recv.at[2], device)
    for half in range(2):
        qr[half, me] = qs[me, half]

    @pl.when(first)
    def _():
        for chip in range(CHIPS):
            remote(qs.at[chip, 1 - c], q_first, first_send.at[0], first_recv.at[0], across(chip))

    settle(rs.at[pl.ds(0, Z - 1)], z_recv.at[0])
    total = rs[0]
    for k in range(1, Z):
        total = total + rs[k]
    mine[...] = total
    for d in FAR_Z:
        device = along_z(d)[1]
        remote(mine, ag.at[z], z_send.at[1], z_recv.at[1], device)
    ag[z] = total
    chip_row = lax.broadcasted_iota(jnp.int32, (CHIPS, DOCS), 0)
    chosen = jnp.where(owner[...] == chip_row * Z + z, 1.0, 0.0).astype(BF16)
    settle(qr.at[:, pl.ds(0, CHIPS - 1)], x_recv.at[2])
    for n, half in enumerate((c, 1 - c)):
        for k in range(CHIPS):
            hi, lo = split(qr[half, k])
            qcat[n, 16 * k : 16 * k + 16, 0:128] = hi
            qcat[n, 16 * k : 16 * k + 16, 128:256] = lo
    settle(q_first, first_recv.at[0])
    for n, rows_in in enumerate((qr[c, 0], q_first[...])):
        hi, lo = split(rows_in)
        qcat_first[16 * n : 16 * n + 16, 0:128] = hi
        qcat_first[16 * n : 16 * n + 16, 128:256] = lo
    settle(ag.at[pl.ds(0, Z - 1)], z_recv.at[1])

    ag_copy = to_sibling(3, ag, ag_sib)

    def score(n, table):
        grads = table[...].reshape(128, DOCS)
        hi, lo = split(grads)
        twice = jnp.concatenate([hi, hi], axis=0)
        row_part = lax.dot_general(chosen, hi, NT, preferred_element_type=F32) + lax.dot_general(
            chosen, lo, NT, preferred_element_type=F32
        )
        squares = jnp.sum(grads * grads, axis=0, keepdims=True)
        if n == 0:
            early = dot(qcat_first[...], twice) + dot(qcat_first[:, 0:128], lo)
            for k in range(2):
                f_first[k, 0:16] = early[16 * k : 16 * k + 16]
                f_first[k, 16:17] = squares
                f_first[k, 17:18] = row_part[0:1]
            slot = me * 2 + c

            @pl.when(first)
            def _():
                fr_first[slot] = f_first[0]

            @pl.when(jnp.logical_not(first))
            def _():
                remote(f_first.at[0], fr_first.at[slot], first_send.at[1], first_recv.at[1], (z, c))

            remote(f_first.at[1], fr_first.at[slot], first_send.at[2], first_recv.at[1], (z, 1 - c))
        part_scores = dot(qcat[n], twice) + dot(qcat[n, :, 0:128], lo)
        return part_scores, squares, row_part

    own_scores, own_squares, own_row = score(0, ag)
    ag_copy.wait_recv()
    sib_scores, sib_squares, sib_row = score(1, ag_sib)
    both_scores = own_scores + sib_scores
    squares = own_squares + sib_squares
    first_core = c == 0
    row_0 = jnp.where(first_core, own_row, sib_row)
    row_1 = jnp.where(first_core, sib_row, own_row)
    for k in range(CHIPS):
        fs[k, 0:16] = both_scores[16 * k : 16 * k + 16]
        fs[k, 16:17] = squares
        fs[k, 17:18] = row_0[k : k + 1]
        fs[k, 18:19] = row_1[k : k + 1]
    for o in FAR:
        chip, device = peer(o)

        @pl.when(me != o)
        def _():
            remote(fs.at[chip], fr.at[me], x_send.at[3], x_recv.at[3], device)

    def results(parts, row):
        summed = parts(0)
        for k in range(1, row[0]):
            summed = summed + parts(k)
        inverse = 1.0 / jnp.sqrt(summed[16:17] * (1.0 / COLS) + 1e-06)
        scores[...] = summed[0:16] * inverse
        own = jnp.sum(jnp.where(owner[...] == s, inverse, 0.0), axis=1, keepdims=True)
        lanes = lax.broadcasted_iota(jnp.int32, (8, 128), 1) // 16
        tiles = [
            jnp.concatenate([row[1]((bi // 2) * Y + bj, bi % 2) for bi in range(8)], axis=0) * own
            for bj in range(4)
        ]
        for p in range(4):
            pick = (lanes + (4 - p)) % 4
            out = tiles[3]
            for bj in range(3):
                out = jnp.where(pick == bj, tiles[bj], out)
            if p:
                out = pltpu.roll(out, 128 - 16 * p, 1)
            for bi in range(8):
                store[0:1, (bi * 4 + p) * 128 : (bi * 4 + p + 1) * 128] = out[bi : bi + 1]

    for copy in (sib_copies[0], sib_copies[1], g_copy, ag_copy):
        copy.wait_send()
    settle(xr.at[pl.ds(0, CHIPS - 1)], x_send.at[0])
    settle(xl.at[pl.ds(0, CHIPS - 1)], x_send.at[1])
    settle(qr.at[:, pl.ds(0, CHIPS - 1)], x_send.at[2])
    settle(rs.at[pl.ds(0, Z - 1)], z_send.at[0])
    settle(ag.at[pl.ds(0, Z - 1)], z_send.at[1])
    settle(f_first.at[1], first_send.at[2])

    @pl.when(first)
    def _():
        settle(qs.at[:, 0], first_send.at[0])
        settle(fr.at[pl.ds(0, CHIPS - 1)], x_send.at[3])
        settle(fr_first.at[pl.ds(0, 2 * CHIPS - 1)], first_recv.at[1])
        results(lambda k: fr_first[k], (2 * CHIPS, lambda chip, half: fr_first[2 * chip + half, 17:18, :]))

    @pl.when(jnp.logical_not(first))
    def _():
        fr[me] = fs[me]
        settle(f_first.at[0], first_send.at[1])
        settle(fr.at[pl.ds(0, CHIPS - 2)], x_send.at[3])
        settle(fr.at[pl.ds(0, CHIPS - 1)], x_recv.at[3])
        results(lambda k: fr[k], (CHIPS, lambda chip, half: fr[chip, 17 + half : 18 + half, :]))


def finish(row, partial, store, scores):
    store[...] = row[...]
    scores[...] = partial[...]


def per_device(hidden_acts, out_grads, proj_in, proj_out, doc_lengths, owner, queries):
    anywhere = pl.BlockSpec(memory_space=pl.ANY)
    vmem = pl.BlockSpec(memory_space=pltpu.VMEM)
    width, model = hidden_acts.shape[1], out_grads.shape[1]
    dma = pltpu.SemaphoreType.DMA
    row, partial = pl.pallas_call(
        kernel,
        out_shape=(jax.ShapeDtypeStruct((1, COLS), F32), jax.ShapeDtypeStruct((16, DOCS), F32)),
        in_specs=[anywhere] * 7,
        out_specs=(vmem, vmem),
        scratch_shapes=[
            pltpu.VMEM((TOK, width), BF16),
            pltpu.VMEM((TOK, model), BF16),
            pltpu.VMEM((RANK, width), BF16),
            pltpu.VMEM((RANK, model), BF16),
            pltpu.VMEM((1, DOCS), jnp.int32),
            pltpu.VMEM((1, DOCS), jnp.int32),
            pltpu.VMEM((16, COLS), F32),
            pltpu.VMEM((2, TOK, RANK), F32),
            pltpu.VMEM((2, RANK, HALF), F32),
            pltpu.VMEM((2, RANK, HALF), F32),
            pltpu.VMEM((RANK, HALF), F32),
            pltpu.VMEM((RANK, HALF), F32),
            pltpu.VMEM((CHIPS, 16, HALF), F32),
            pltpu.VMEM((CHIPS, 16, HALF), F32),
            pltpu.VMEM((CHIPS * HALF, DOCS), BF16),
            pltpu.VMEM((2, 2, 8, 16, CHIPS * HALF), BF16),
            pltpu.VMEM((CHIPS, 2, 16, 128), F32),
            pltpu.VMEM((2, CHIPS, 16, 128), F32),
            pltpu.VMEM((2, CHIPS * 16, 256), BF16),
            pltpu.VMEM((128, DOCS), F32),
            pltpu.VMEM((128, DOCS), F32),
            pltpu.VMEM((128, DOCS), F32),
            pltpu.VMEM((Z, 16, DOCS), F32),
            pltpu.VMEM((16, DOCS), F32),
            pltpu.VMEM((Z, 16, DOCS), F32),
            pltpu.VMEM((Z, 16, DOCS), F32),
            pltpu.VMEM((CHIPS, 19, DOCS), F32),
            pltpu.VMEM((CHIPS, 19, DOCS), F32),
            pltpu.VMEM((16, 128), F32),
            pltpu.VMEM((32, 256), BF16),
            pltpu.VMEM((2, 18, DOCS), F32),
            pltpu.VMEM((2 * CHIPS, 18, DOCS), F32),
            dma((18,)),
            dma((4,)),
            dma((4,)),
            dma((4,)),
            dma((4,)),
            dma((2,)),
            dma((2,)),
            dma((3,)),
            dma((2,)),
        ],
        compiler_params=pltpu.CompilerParams(
            collective_id=1, has_side_effects=True, vmem_limit_bytes=40 << 20
        ),
        name="influence",
    )(
        *[
            pltpu.with_memory_space_constraint(v, pltpu.HBM)
            for v in (hidden_acts, out_grads, proj_in.T, proj_out.T, doc_lengths[None], owner[None], queries)
        ]
    )
    return pl.pallas_call(
        finish,
        out_shape=(jax.ShapeDtypeStruct(row.shape, F32), jax.ShapeDtypeStruct(partial.shape, F32)),
        in_specs=[vmem] * 2,
        out_specs=(vmem, vmem),
        compiler_params=pltpu.CompilerParams(vmem_limit_bytes=1 << 20),
        name="finish",
    )(row, partial)


def solution(mesh):
    in_specs = (
        P("seq", "tp"),
        P("seq", "tp"),
        P("tp", None),
        P("tp", None),
        P(),
        P(),
        P(("seq", "tp"), None),
    )
    out_specs = (P("seq", None), P(("seq", "tp"), None))
    return jax.shard_map(per_device, mesh=mesh, in_specs=in_specs, out_specs=out_specs, check_vma=False)
```
